256 devices in a mesh: dp: 8 (over y, core), proto: 32 (over z, x).
Axes of the slice: x: 4, y: 4, z: 8, core: 2. Of those that a mesh axis runs over, the one named last changes fastest.
Arguments:
- embeddings: bfloat16 [8192, 256], P('dp'), may hold values from -0.375 to 0.375
- queue: bfloat16 [8192, 256], P('dp'), may hold values from -0.375 to 0.375
- prototypes: bfloat16 [256, 65536], P(None, 'proto'), may hold values from -0.375 to 0.375
- pairing: int32 [8192], P('dp'), may hold values from 0 to 8191, as said below
Outputs:
- grad_embed: float32 [8192, 256], P('dp')
- grad_proto: float32 [256, 65536], P(None, 'proto')
- loss_mean: float32 [], replicated
The draws below stay inside these ranges and needn't reach their ends.
Inputs may be any that keep to these rules, and one draw needn't show every extreme that they name: pairing[pairing[i]] = i and pairing[i] != i; i and pairing[i] lie in the same aligned block of 1024 rows.
All inputs are finite; a program needn't handle non-finite values.
Results may differ from the reference program's by a relative error of at most 0.0011.
The reference program's roundings to bfloat16 on the way (of `embed_bf`, `proto_bf` and `differ`) count: a program that leaves them out, or rounds other values in their place, can miss the bound.
Values sent between devices are 32-bit elements; how exact they have to be, the bound alone decides.
A program may use at most 128 MiB of HBM per device.

```python
import math
import jax
import jax.numpy as jnp
from jax import lax

D = 256
PROTOS = 65536
ITERS = 3
CROP_DEV = 1024
CROPS = 8192
QUEUE = 8192
ROWS = 16384


def shared_direction(key):
    return jnp.where(jax.random.bernoulli(key, 0.5, (D,)), 1.0, -1.0).astype(jnp.float32)


def draw_embeddings(key, part):
    direction = shared_direction(key)
    key = jax.random.fold_in(key, 11)
    noise_key, along_key = jax.random.split(key)
    noise_part = jnp.clip(jax.random.normal(noise_key, (CROPS, D)), -5.0, 5.0)
    along_part = jax.random.uniform(along_key, (CROPS, 1), minval=-0.6, maxval=0.6)
    return ((noise_part + along_part * direction[None, :]) / math.sqrt(D)).astype(jnp.bfloat16)


def draw_queue(key, part):
    direction = shared_direction(key)
    key = jax.random.fold_in(key, 23)
    noise_key, along_key = jax.random.split(key)
    noise_part = jnp.clip(jax.random.normal(noise_key, (QUEUE, D)), -5.0, 5.0)
    along_part = jax.random.uniform(along_key, (QUEUE, 1), minval=-0.6, maxval=0.6)
    return ((noise_part + along_part * direction[None, :]) / math.sqrt(D)).astype(jnp.bfloat16)


def draw_prototypes(key, part):
    direction = shared_direction(key)
    key = jax.random.fold_in(key, 37)
    noise_key, along_key = jax.random.split(key)
    noise_part = jnp.clip(jax.random.normal(noise_key, (D, PROTOS)), -5.0, 5.0)
    along_part = jax.random.uniform(along_key, (1, PROTOS), minval=-0.6, maxval=0.6)
    return ((noise_part + along_part * direction[:, None]) / math.sqrt(D)).astype(jnp.bfloat16)


def draw_pairing(key, part):
    key = jax.random.fold_in(key, 53)
    block_count = CROPS // CROP_DEV

    def one_block(block_key, block_index):
        order = jax.random.permutation(block_key, CROP_DEV).astype(jnp.int32)
        evens = order[0::2]
        odds = order[1::2]
        partner = jnp.zeros((CROP_DEV,), jnp.int32).at[evens].set(odds).at[odds].set(evens)
        return partner + block_index * CROP_DEV
    keys = jax.random.split(key, block_count)
    blocks = jax.vmap(one_block)(keys, jnp.arange(block_count, dtype=jnp.int32))
    return blocks.reshape(CROPS).astype(jnp.int32)


def setup_inputs(seed: int = 0) -> dict:
    key_of = jax.random.split(jax.random.key(seed), 5)
    embeddings = draw_embeddings(jax.random.fold_in(key_of[4], 71), 0)
    queue = draw_queue(jax.random.fold_in(key_of[4], 71), 0)
    prototypes = draw_prototypes(jax.random.fold_in(key_of[4], 71), 0)
    pairing = draw_pairing(jax.random.fold_in(key_of[4], 71), 0)
    return dict(embeddings=embeddings, queue=queue, prototypes=prototypes, pairing=pairing)


EPS_SINK = 0.05
TEMPER = 0.1
HIGHEST_PREC = lax.Precision.HIGHEST

def unit_rows(values):
    return values * lax.rsqrt(lax.optimization_barrier(jnp.sum(values * values, axis=1, keepdims=True)) + 1e-06)

def unit_cols(values):
    return values * lax.rsqrt(lax.optimization_barrier(jnp.sum(values * values, axis=0, keepdims=True)) + 1e-06)

def reference(embeddings, queue, prototypes, pairing):
    embed_unit, embed_back = jax.vjp(unit_rows, embeddings.astype(jnp.float32))
    proto_unit, proto_back = jax.vjp(unit_cols, prototypes.astype(jnp.float32))
    embed_bf = embed_unit.astype(jnp.bfloat16)
    queue_bf = unit_rows(queue.astype(jnp.float32)).astype(jnp.bfloat16)
    proto_bf = proto_unit.astype(jnp.bfloat16)
    all_rows = jnp.concatenate([embed_bf, queue_bf], axis=0)
    block_width = min(PROTOS, 2048)
    block_count = PROTOS // block_width
    proto_blocks = proto_bf.reshape(D, block_count, block_width).transpose(1, 0, 2)
    row_scale = jnp.ones((ROWS,), jnp.float32)
    col_blocks = jnp.zeros((block_count, block_width), jnp.float32)
    for sweep_index in range(ITERS):

        def sweep_fn(running, block_cols):
            exponent = jnp.exp(jnp.dot(all_rows, block_cols, preferred_element_type=jnp.float32) / EPS_SINK)
            block_scale = 1.0 / (PROTOS * jnp.dot(row_scale, exponent, precision=HIGHEST_PREC))
            return (running + jnp.dot(exponent, block_scale, precision=HIGHEST_PREC), block_scale)
        summed, col_blocks = lax.scan(sweep_fn, jnp.zeros((ROWS,), jnp.float32), proto_blocks)
        row_scale = 1.0 / (ROWS * summed)
    partner_embed = embed_bf[pairing]
    partner_scale = (row_scale[:CROPS] * ROWS)[pairing]

    def block_codes(block_cols, block_scale):
        scores_crop = jnp.dot(embed_bf, block_cols, preferred_element_type=jnp.float32)
        partner_exp = jnp.exp(jnp.dot(partner_embed, block_cols, preferred_element_type=jnp.float32) / EPS_SINK)
        codes = partner_exp * block_scale[None, :] * partner_scale[:, None]
        return (scores_crop, codes)

    def stats_fn(totals, pieces):
        scores_crop, codes = block_codes(pieces[0], pieces[1])
        return ((totals[0] + lax.optimization_barrier(jnp.sum(jnp.exp(scores_crop / TEMPER), axis=1)), totals[1] + lax.optimization_barrier(jnp.sum(codes * scores_crop, axis=1))), None)
    zeros_crop = jnp.zeros((CROPS,), jnp.float32)
    (soft_total, code_sum), _ = lax.scan(stats_fn, (zeros_crop, zeros_crop), (proto_blocks, col_blocks))
    code_score = code_sum / TEMPER
    cross_ent = jnp.log(soft_total) - code_score
    loss_mean = jnp.sum(cross_ent) / CROPS

    def grad_fn(embed_cot, pieces):
        scores_crop, codes = block_codes(pieces[0], pieces[1])
        soft = jnp.exp(scores_crop / TEMPER) / soft_total[:, None]
        differ = ((soft - codes) / TEMPER).astype(jnp.bfloat16)
        embed_cot = embed_cot + lax.dot_general(differ, pieces[0], (((1,), (1,)), ((), ())), preferred_element_type=jnp.float32)
        proto_piece = lax.dot_general(embed_bf, differ, (((0,), (0,)), ((), ())), preferred_element_type=jnp.float32)
        return (embed_cot, proto_piece)
    embed_cot, proto_pieces = lax.scan(grad_fn, jnp.zeros((CROPS, D), jnp.float32), (proto_blocks, col_blocks))
    proto_cot = proto_pieces.transpose(1, 0, 2).reshape(D, PROTOS)
    grad_embed = math.sqrt(PROTOS) * embed_back(embed_cot)[0]
    grad_proto = PROTOS / math.sqrt(CROPS) * proto_back(proto_cot)[0]
    return (grad_embed, grad_proto, loss_mean)
```

```python
import functools
import math

import jax
import jax.numpy as jnp
from jax import lax
from jax.experimental import pallas as pl
from jax.experimental.pallas import tpu as pltpu
from jax.sharding import PartitionSpec as P

PROTOS = 65536
ITERS = 3
CORES = 2
ALONG_X = 4
LOG2E = math.log2(math.e)
F32 = jnp.float32
BF16 = jnp.bfloat16
MESH = pl.DeviceIdType.MESH


def inv_norm(sum_sq):
    shifted = sum_sq + 1e-06
    guess = lax.rsqrt(shifted)
    return guess * (1.5 - 0.5 * shifted * guess * guess)


def aligned(index, size):
    return pl.ds(pl.multiple_of(index * size, size), size)


class Exchange:
    def __init__(self, buf, send_sem, recv_sem, me, size, device):
        self.buf, self.me, self.size, self.device = buf, me, size, device
        self.send_sem, self.recv_sem = send_sem, recv_sem

    def copy(self, hop, slot):
        return pltpu.make_async_remote_copy(
            src_ref=self.buf.at[self.me],
            dst_ref=self.buf.at[slot],
            send_sem=self.send_sem.at[hop],
            recv_sem=self.recv_sem.at[slot],
            device_id=self.device(lax.rem(self.me + hop, self.size)),
            device_id_type=MESH,
        )

    def start(self, block):
        self.buf[self.me] = block
        for hop in range(1, self.size):
            self.copy(hop, self.me).start()

    def finish(self):
        for hop in range(1, self.size):
            self.copy(hop, lax.rem(self.me + hop, self.size)).wait_recv()
        for hop in range(1, self.size):
            self.copy(hop, self.me).wait_send()
        total = self.buf[0]
        for slot in range(1, self.size):
            total = total + self.buf[slot]
        return total


class Ring:
    def __init__(self, n, me, part, recv, send_sem, recv_sem, device):
        self.n, self.me, self.part, self.recv = n, me, part, recv
        self.send_sem, self.recv_sem, self.device = send_sem, recv_sem, device
        self.far = n // 2
        self.sent = []

    def at(self, hops):
        return lax.rem(self.me + hops + self.n, self.n)

    def copy(self, way, step, half, piece):
        return pltpu.make_async_remote_copy(
            src_ref=self.part(piece, half),
            dst_ref=self.recv.at[way, step - 1, half],
            send_sem=self.send_sem.at[way, step - 1, half],
            recv_sem=self.recv_sem.at[way, step - 1, half],
            device_id=self.device(self.at(1 if way == 0 else -1)),
            device_id_type=MESH,
        )

    def send(self, way, step, half, piece):
        copy = self.copy(way, step, half, piece)
        copy.start()
        self.sent.append(copy)

    def take(self, way, step, half, piece):
        self.copy(way, step, half, piece).wait_recv()
        view = self.part(piece, half)
        view[...] = view[...] + self.recv[way, step - 1, half]

    def target(self, way, step):
        hops = self.far - step + 1
        return self.at(hops if way == 0 else -hops)

    def first(self):
        if self.n > 1:
            for way in range(2):
                self.send(way, 1, way, self.at(self.far))

    def early(self, way):
        if self.far >= 2:
            self.send(way, 2, 1 - way, self.target(way, 2))

    def second(self):
        if self.far >= 2:
            for way in range(2):
                piece = self.target(way, 2)
                self.take(way, 1, way, piece)
                self.send(way, 2, way, piece)

    def step(self, step):
        if 2 < step <= self.far:
            for way in range(2):
                piece = self.target(way, step)
                for half in (way, 1 - way):
                    self.take(way, step - 1, half, piece)
                    self.send(way, step, half, piece)

    def finish(self):
        if self.n == 2:
            for way in range(2):
                self.take(way, 1, way, self.me)
        elif self.n > 2:
            for way in range(2):
                for half in range(2):
                    self.take(way, self.far, half, self.me)

    def close(self):
        for copy in self.sent:
            copy.wait_send()


class Gather:
    def __init__(self, n, me, view, send_sem, recv_sem, device):
        self.n, self.me, self.view = n, me, view
        self.send_sem, self.recv_sem, self.device = send_sem, recv_sem, device
        self.far = n // 2
        self.sent = []

    def at(self, hops):
        return lax.rem(self.me + hops + self.n, self.n)

    def halves(self, way, hops):
        return (way, 1 - way) if hops < self.far else (way,)

    def copy(self, way, hops, half, piece):
        return pltpu.make_async_remote_copy(
            src_ref=self.view(piece, half),
            dst_ref=self.view(piece, half),
            send_sem=self.send_sem.at[way, hops - 1, half],
            recv_sem=self.recv_sem.at[way, hops - 1, half],
            device_id=self.device(self.at(1 if way == 0 else -1)),
            device_id_type=MESH,
        )

    def source(self, way, hops):
        return self.at(-hops if way == 0 else hops)

    def forward(self, way, hops):
        if hops <= self.far:
            piece = self.source(way, hops - 1)
            for half in self.halves(way, hops):
                copy = self.copy(way, hops, half, piece)
                copy.start()
                self.sent.append(copy)

    def first(self):
        if self.n > 1:
            for way in range(2):
                self.forward(way, 1)

    def take(self, way, hops):
        if 1 <= hops <= self.far:
            piece = self.source(way, hops)
            for half in self.halves(way, hops):
                self.copy(way, hops, half, piece).wait_recv()
                if hops < self.far and half in self.halves(way, hops + 1):
                    copy = self.copy(way, hops + 1, half, piece)
                    copy.start()
                    self.sent.append(copy)

    def rest(self):
        for hops in range(1, self.far + 1):
            for way in range(2):
                self.take(way, hops)

    def close(self):
        for copy in self.sent:
            copy.wait_send()


def kernel(
    sizes,
    emb,
    que,
    pro,
    pair,
    out_e,
    out_p,
    out_l,
    ex,
    sx,
    yx,
    rows_bf,
    part_bf,
    pro_bf,
    emb_t,
    pro_t,
    differ,
    colacc,
    lanes,
    softp,
    rbc,
    stb,
    qpart,
    dpbuf,
    xbuf,
    zbuf,
    ldp,
    lx,
    lz,
    pc,
    sib,
    yrecv,
    ag,
    h1,
    h2,
    x1recv,
    z1recv,
    z2recv,
    x2recv,
    e1,
    e2,
    dp_sems,
    x_sems,
    z_sems,
    ldp_sems,
    lx_sems,
    lz_sems,
    sib_sems,
    y_sems,
    x1_sems,
    z1_sems,
    z2_sems,
    x2_sems,
    yg_sems,
    sg_sems,
    z1g_sems,
    x1g_sems,
    x2g_sems,
    z2g_sems,
    op_sems,
    oe_sems,
):
    ny, nx, nz = sizes
    dp_count = ny * CORES
    crops, depth = emb.shape
    rows = crops + que.shape[0]
    cols = pro.shape[1]
    total_rows = rows * dp_count
    total_crops = crops * dp_count
    lane_blocks = cols // 128
    row_blocks = rows // 128
    crop_blocks = crops // 128
    width = cols // dp_count
    tile = 256

    my_dp = lax.axis_index("dp")
    my_proto = lax.axis_index("proto")
    my_y, my_c = my_dp // CORES, lax.rem(my_dp, CORES)
    my_z, my_x = my_proto // nx, lax.rem(my_proto, nx)

    def on_dp(index):
        return (index, my_proto)

    def on_x(index):
        return (my_dp, my_z * nx + index)

    def on_z(index):
        return (my_dp, index * nx + my_x)

    def on_y(index):
        return (index * CORES + my_c, my_proto)

    sibling = (my_y * CORES + 1 - my_c, my_proto)

    barrier = pltpu.get_barrier_semaphore()
    for me, size, device in ((my_dp, dp_count, on_dp), (my_x, nx, on_x), (my_z, nz, on_z)):
        for hop in range(1, size):
            pl.semaphore_signal(
                barrier, inc=1, device_id=device(lax.rem(me + hop, size)), device_id_type=MESH
            )

    @pl.loop(0, crops // tile)
    def _(i):
        block = aligned(i, tile)
        for source, first in ((emb, 0), (que, crops)):
            values = source[block, :].astype(F32)
            inv = inv_norm(jnp.sum(values * values, axis=1, keepdims=True))
            start = pl.multiple_of(first + i * tile, tile)
            rows_bf[pl.ds(start, tile), :] = (values * inv).astype(BF16)

    @pl.loop(0, cols // tile)
    def _(j):
        block = aligned(j, tile)
        values = pro[:, block].astype(F32)
        inv = inv_norm(jnp.sum(values * values, axis=0, keepdims=True))
        pro_bf[:, block] = (values * inv).astype(BF16)

    softp[...] = jnp.zeros_like(softp)

    @pl.loop(0, cols // tile)
    def _(j):
        block = aligned(j, tile)
        weights = pro_bf[:, block]
        acc = jnp.zeros((8, tile), F32)
        for i in range(rows // tile):
            lines = slice(i * tile, (i + 1) * tile)
            scores = jnp.dot(rows_bf[lines, :], weights, preferred_element_type=F32)
            if i < crops // tile:
                sx[lines, block] = scores
                soft = jnp.exp2(scores * (10.0 * LOG2E))
                folded = soft[:, :128]
                for k in range(1, tile // 128):
                    folded = folded + soft[:, k * 128 : (k + 1) * 128]
                softp[lines, :] += folded
                expo = soft * soft
            else:
                expo = jnp.exp2(scores * (20.0 * LOG2E))
            ex[lines, block] = expo
            acc = acc + jnp.sum(expo.reshape(tile // 8, 8, tile), axis=0)
        colacc[j] = acc

    def dense_cols():
        pieces = []
        for j in range(lane_blocks):
            k, part = j * 128 // tile, (j * 128) % tile
            pieces.append(jnp.sum(colacc[k, :, part : part + 128], axis=0, keepdims=True))
        return jnp.concatenate(pieces, axis=0)

    def dense_rows(source, blocks):
        pieces = []
        for b in range(blocks):
            pieces.append(
                jnp.sum(source[b * 128 : (b + 1) * 128, :].T, axis=0, keepdims=True)
            )
        return jnp.concatenate(pieces, axis=0)

    def spread_rows(target, dense, blocks):
        for b in range(blocks):
            target[b * 128 : (b + 1) * 128, :] = jnp.broadcast_to(
                dense[b : b + 1, :], (128, 128)
            ).T

    def col_pass():
        groups = 4

        def step(i, accs):
            accs = list(accs)
            for g in range(groups):
                lines = pl.ds(pl.multiple_of(i * 8 * groups + 8 * g, 8), 8)
                scale = rbc[lines, :]
                for j in range(lane_blocks):
                    accs[j] = accs[j] + ex[lines, j * 128 : (j + 1) * 128] * scale
            return tuple(accs)

        accs = lax.fori_loop(
            0, rows // (8 * groups), step, (jnp.zeros((8, 128), F32),) * lane_blocks
        )
        return jnp.concatenate([jnp.sum(a, axis=0, keepdims=True) for a in accs], axis=0)

    def spread_cols(dense):
        return [
            jnp.broadcast_to(dense[j : j + 1, :], (8, 128)) for j in range(lane_blocks)
        ]

    def row_pass(scales):
        groups = 4

        @pl.loop(0, rows // (8 * groups))
        def _(i):
            for g in range(groups):
                lines = pl.ds(pl.multiple_of(i * 8 * groups + 8 * g, 8), 8)
                acc = ex[lines, :128] * scales[0]
                for j in range(1, lane_blocks):
                    acc = acc + ex[lines, j * 128 : (j + 1) * 128] * scales[j]
                lanes[lines, :] = acc

    def partner_pass(scales):
        groups = 4

        @pl.loop(0, crops // (8 * groups))
        def _(i):
            for g in range(groups):
                lines = pl.ds(pl.multiple_of(i * 8 * groups + 8 * g, 8), 8)
                acc = jnp.zeros((8, 128), F32)
                for j in range(lane_blocks):
                    block = slice(j * 128, (j + 1) * 128)
                    code = yx[lines, block] * scales[j]
                    yx[lines, block] = code
                    acc = acc + code
                lanes[lines, :] = acc

    def soften(first, last):
        groups = 2

        @pl.loop(first // (8 * groups), last // (8 * groups))
        def _(i):
            for g in range(groups):
                lines = pl.ds(pl.multiple_of(i * 8 * groups + 8 * g, 8), 8)
                scale = stb[lines, :]
                acc = jnp.zeros((8, 128), F32)
                for j in range(lane_blocks):
                    block = slice(j * 128, (j + 1) * 128)
                    score = sx[lines, block]
                    acc = acc + yx[lines, block] * score
                    sx[lines, block] = jnp.exp2(score * (10.0 * LOG2E)) * scale
                qpart[lines, :] = acc

    def partners():
        local_pair = pair[...] - my_dp * crops

        @pl.loop(0, crops // tile)
        def _(i):
            block = aligned(i, tile)
            line = lax.broadcasted_iota(jnp.int32, (tile, crops), 0) + i * tile
            pick = jnp.where(line == local_pair, 1.0, 0.0).astype(BF16)
            part_bf[block, :] = jnp.dot(
                pick, rows_bf[:crops, :], preferred_element_type=F32
            ).astype(BF16)

        @pl.loop(0, cols // tile)
        def _(j):
            block = aligned(j, tile)
            weights = pro_bf[:, block]
            for i in range(crops // tile):
                lines = slice(i * tile, (i + 1) * tile)
                scores = jnp.dot(part_bf[lines, :], weights, preferred_element_type=F32)
                soft = jnp.exp2(scores * (10.0 * LOG2E))
                yx[lines, block] = soft * soft

    def transposed_rows():
        @pl.loop(0, crops // tile)
        def _(i):
            block = aligned(i, tile)
            emb_t[:, block] = rows_bf[block, :].astype(F32).T.astype(BF16)

    def transposed_cols():
        @pl.loop(0, cols // tile)
        def _(j):
            block = aligned(j, tile)
            pro_t[block, :] = pro_bf[:, block].astype(F32).T.astype(BF16)

    pl.semaphore_wait(barrier, dp_count - 1 + nx - 1 + nz - 1)
    col_dense = dense_cols()
    soft_total = None
    row_sum = None
    for it in range(ITERS):
        over_dp = Exchange(
            dpbuf.at[it], dp_sems.at[it, 0], dp_sems.at[it, 1], my_dp, dp_count, on_dp
        )
        over_x = Exchange(
            xbuf.at[it], x_sems.at[it, 0], x_sems.at[it, 1], my_x, nx, on_x
        )
        over_z = Exchange(
            zbuf.at[it], z_sems.at[it, 0], z_sems.at[it, 1], my_z, nz, on_z
        )
        over_dp.start(col_dense)
        if it == 0:
            partners()
        elif it == 1:
            spread_rows(stb, 10.0 / soft_total, crop_blocks)
        elif it == 2:
            transposed_cols()
        col_scale = 1.0 / (PROTOS * over_dp.finish())
        blank = jnp.zeros((crop_blocks, 128), F32)
        if it < ITERS - 1:
            row_pass(spread_cols(col_scale))
            extra = dense_rows(softp, crop_blocks) if it == 0 else blank
            block = jnp.concatenate([dense_rows(lanes, row_blocks), extra], axis=0)
            over_x.start(block)
            if it == 0:
                transposed_rows()
            over_z.start(over_x.finish())
            total = over_z.finish()
            if it == 0:
                soft_total = total[row_blocks:, :]
            spread_rows(rbc, 1.0 / (total_rows * total[:row_blocks, :]), row_blocks)
            col_dense = col_pass()
        else:
            partner_pass(spread_cols(10.0 * col_scale))
            filler = jnp.zeros((row_blocks, 128), F32)
            over_x.start(
                jnp.concatenate([dense_rows(lanes, crop_blocks), filler], axis=0)
            )
            soften(0, crops // 2)
            over_z.start(over_x.finish())
            soften(crops // 2, crops)
            row_sum = over_z.finish()[:crop_blocks, :]

    spread_rows(rbc, 10.0 / row_sum, crop_blocks)

    def add_up(i, acc):
        lines = aligned(i, 8)
        return acc + qpart[lines, :] * rbc[lines, :]

    code_score = lax.fori_loop(0, crops // 8, add_up, jnp.zeros((8, 128), F32))
    log_total = jnp.log(soft_total) * (1.0 / (nx * nz))
    if crop_blocks != 8:
        log_total = jnp.broadcast_to(jnp.sum(log_total, axis=0, keepdims=True), (8, 128)) / 8.0
    loss_dp = Exchange(ldp, ldp_sems.at[0], ldp_sems.at[1], my_dp, dp_count, on_dp)
    loss_x = Exchange(lx, lx_sems.at[0], lx_sems.at[1], my_x, nx, on_x)
    loss_z = Exchange(lz, lz_sems.at[0], lz_sems.at[1], my_z, nz, on_z)
    loss_dp.start(log_total - code_score)

    def piece(t, core):
        block = aligned(t * CORES + core, width)
        for i in range(crops // tile):
            lines = slice(i * tile, (i + 1) * tile)
            scale = rbc[lines, :]
            scale = jnp.concatenate([scale] * (width // 128), axis=1)
            value = sx[lines, block] - yx[lines, block] * scale
            differ[lines, block] = value.astype(BF16)
        cot = jnp.dot(emb_t[...], differ[:, block], preferred_element_type=F32)
        half = depth // 2
        pc[t, core, 0] = cot[:half, :]
        pc[t, core, 1] = cot[half:, :]

    def to_sibling(order, t):
        return pltpu.make_async_remote_copy(
            src_ref=pc.at[t, 1 - my_c],
            dst_ref=sib.at[order],
            send_sem=sib_sems.at[0, order],
            recv_sem=sib_sems.at[1, order],
            device_id=sibling,
            device_id_type=MESH,
        )

    y_ring = Ring(
        ny,
        my_y,
        lambda t, half: pc.at[t, my_c, half],
        yrecv,
        y_sems.at[0],
        y_sems.at[1],
        on_y,
    )
    near = [] if ny < 4 else [1, -1]
    order = ([ny // 2] if ny > 1 else []) + near + [0]
    for number, hops in enumerate(order):
        t = y_ring.at(hops)
        piece(t, 1 - my_c)
        to_sibling(number, t).start()
        piece(t, my_c)
        to_sibling(number, t).wait_recv()
        pc[t, my_c] = pc[t, my_c] + sib[number]
        if number == 0 and ny > 1:
            y_ring.first()
        elif hops == 1:
            y_ring.early(0)
        elif hops == -1:
            y_ring.early(1)

    share = crops // (nx * nz)
    for px in range(nx):
        lines = slice(px * nz * share, (px + 1) * nz * share)
        cot = jnp.dot(differ[lines, :], pro_t[...], preferred_element_type=F32)
        for pz in range(nz):
            h1[px, pz] = cot[pz * share : (pz + 1) * share, :128]
            h2[pz, px] = cot[pz * share : (pz + 1) * share, 128:]

    zh, xh, sh = max(nz // 2, 1), max(nx // 2, 1), share // 2
    x1 = Ring(
        nx,
        my_x,
        lambda t, half: h1.at[t, pl.ds(half * zh, zh)],
        x1recv,
        x1_sems.at[0],
        x1_sems.at[1],
        on_x,
    )
    z1 = Ring(
        nz,
        my_z,
        lambda t, half: h1.at[my_x, t, pl.ds(half * sh, sh)],
        z1recv,
        z1_sems.at[0],
        z1_sems.at[1],
        on_z,
    )
    z2 = Ring(
        nz,
        my_z,
        lambda t, half: h2.at[t, pl.ds(half * xh, xh)],
        z2recv,
        z2_sems.at[0],
        z2_sems.at[1],
        on_z,
    )
    x2 = Ring(
        nx,
        my_x,
        lambda t, half: h2.at[my_z, t, pl.ds(half * sh, sh)],
        x2recv,
        x2_sems.at[0],
        x2_sems.at[1],
        on_x,
    )
    for ring in (x1, z2):
        ring.first()
        ring.early(0)
        ring.early(1)
    y_ring.second()
    x1.second()
    z2.second()
    loss_x.start(loss_dp.finish())
    z2.step(3)
    x1.finish()
    z1.first()
    z1.early(0)
    z1.early(1)
    z2.step(4)
    z1.second()
    z1.step(3)
    loss_z.start(loss_x.finish())
    y_ring.finish()

    half = depth // 2
    block = aligned(my_dp, width)
    values = pro[:, block].astype(F32)
    inv = inv_norm(jnp.sum(values * values, axis=0, keepdims=True))
    cots = [pc[my_y, my_c, 0], pc[my_y, my_c, 1]]
    along = jnp.sum(cots[0] * values[:half, :], axis=0, keepdims=True) + jnp.sum(
        cots[1] * values[half:, :], axis=0, keepdims=True
    )
    factor = PROTOS / math.sqrt(total_crops)
    pull = along * (inv * inv * inv) * factor
    scale = inv * factor
    ag[my_y, my_c, 0] = cots[0] * scale - values[:half, :] * pull
    ag[my_y, my_c, 1] = cots[1] * scale - values[half:, :] * pull
    y_gather = Gather(
        ny,
        my_y,
        lambda t, part: ag.at[t, my_c, part],
        yg_sems.at[0],
        yg_sems.at[1],
        on_y,
    )
    y_gather.first()

    def share_copy(number, t, core):
        return pltpu.make_async_remote_copy(
            src_ref=ag.at[t, core],
            dst_ref=ag.at[t, core],
            send_sem=sg_sems.at[0, number],
            recv_sem=sg_sems.at[1, number],
            device_id=sibling,
            device_id_type=MESH,
        )

    def out_copy(number, t, core):
        return pltpu.make_async_copy(
            ag.at[t, core],
            out_p.at[:, :, aligned(t * CORES + core, width)],
            op_sems.at[core_slot(core), number],
        )

    def core_slot(core):
        return lax.rem(core + my_c, CORES)

    share_order = [0] + [-h for h in near] + ([ny // 2] if ny > 1 else [])

    def hand_on(number):
        t = y_ring.at(share_order[number])
        share_copy(number, t, my_c).start()
        out_copy(number, t, my_c).start()

    hand_on(0)

    z2.finish()
    x2.first()
    x2.early(0)
    x2.early(1)
    z1.step(4)
    x2.second()
    z1.finish()
    x2.finish()
    mine = pl.ds(pl.multiple_of((my_x * nz + my_z) * share, share), share)
    values = emb[mine, :].astype(F32)
    inv = inv_norm(jnp.sum(values * values, axis=1, keepdims=True))
    cots = [h1[my_x, my_z], h2[my_z, my_x]]
    along = jnp.sum(cots[0] * values[:, :128] + cots[1] * values[:, 128:], axis=1, keepdims=True)
    factor = math.sqrt(PROTOS)
    pull = along * (inv * inv * inv) * factor
    scale = inv * factor
    e1[my_x, my_z] = cots[0] * scale - values[:, :128] * pull
    e2[my_z, my_x] = cots[1] * scale - values[:, 128:] * pull
    z1g = Gather(
        nz,
        my_z,
        lambda t, part: e1.at[my_x, t, pl.ds(part * sh, sh)],
        z1g_sems.at[0],
        z1g_sems.at[1],
        on_z,
    )
    x1g = Gather(
        nx,
        my_x,
        lambda t, part: e1.at[t, pl.ds(part * zh, zh)],
        x1g_sems.at[0],
        x1g_sems.at[1],
        on_x,
    )
    x2g = Gather(
        nx,
        my_x,
        lambda t, part: e2.at[my_z, t, pl.ds(part * sh, sh)],
        x2g_sems.at[0],
        x2g_sems.at[1],
        on_x,
    )
    z2g = Gather(
        nz,
        my_z,
        lambda t, part: e2.at[t, pl.ds(part * xh, xh)],
        z2g_sems.at[0],
        z2g_sems.at[1],
        on_z,
    )
    z1g.first()
    x2g.first()
    if ny >= 4:
        y_gather.take(0, 1)
        hand_on(1)
        y_gather.take(1, 1)
        hand_on(2)
    x2g.rest()
    z2g.first()
    z1g.rest()
    x1g.first()
    out_e1 = []

    def write_e1(px):
        return pltpu.make_async_copy(
            e1.at[px], out_e.at[px, :, :, pl.ds(0, 128)], oe_sems.at[0, px]
        )

    def write_e2(pz):
        return pltpu.make_async_copy(
            e2.at[pz], out_e.at[:, pz, :, pl.ds(128, 128)], oe_sems.at[1, pz]
        )

    z2g.take(0, 1)
    z2g.take(1, 1)
    x1g.take(0, 1)
    x1g.take(1, 1)
    z2g.take(0, 2)
    z2g.take(1, 2)
    if ny > 1:
        y_gather.take(0, ny // 2)
        y_gather.take(1, ny // 2)
        hand_on(len(share_order) - 1)
    for hops in range(2, x1g.far + 1):
        x1g.take(0, hops)
        x1g.take(1, hops)
    for px in range(nx):
        write_e1(px).start()
    for hops in range(3, z2g.far + 1):
        z2g.take(0, hops)
        z2g.take(1, hops)
    for pz in range(nz):
        write_e2(pz).start()
    for number in range(len(share_order)):
        t = y_ring.at(share_order[number])
        share_copy(number, t, 1 - my_c).wait_recv()
        out_copy(number, t, 1 - my_c).start()

    out_l[0, 0] = jnp.sum(loss_z.finish()) / total_crops

    for ring in (y_ring, x1, z1, z2, x2, y_gather, z1g, x1g, x2g, z2g):
        ring.close()
    for number, hops in enumerate(order):
        to_sibling(number, y_ring.at(hops)).wait_send()
    for number in range(len(share_order)):
        t = y_ring.at(share_order[number])
        share_copy(number, t, my_c).wait_send()
        out_copy(number, t, my_c).wait()
        out_copy(number, t, 1 - my_c).wait()
    for px in range(nx):
        write_e1(px).wait()
    for pz in range(nz):
        write_e2(pz).wait()


def local(sizes, embeddings, queue, prototypes, pairing):
    ny, nx, nz = sizes
    dp_count = ny * CORES
    crops, depth = embeddings.shape
    rows = crops + queue.shape[0]
    cols = prototypes.shape[1]
    width = cols // dp_count
    share = crops // (nx * nz)
    row_blocks, crop_blocks, lane_blocks = rows // 128, crops // 128, cols // 128
    half = depth // 2
    fy, fx, fz = max(ny // 2, 1), max(nx // 2, 1), max(nz // 2, 1)
    tile = 256
    dma = pltpu.SemaphoreType.DMA
    vmem = pltpu.VMEM
    scratch = [
        vmem((rows, cols), F32),
        vmem((crops, cols), F32),
        vmem((crops, cols), F32),
        vmem((rows, depth), BF16),
        vmem((crops, depth), BF16),
        vmem((depth, cols), BF16),
        vmem((depth, crops), BF16),
        vmem((cols, depth), BF16),
        vmem((crops, cols), BF16),
        vmem((cols // tile, 8, tile), F32),
        vmem((rows, 128), F32),
        vmem((crops, 128), F32),
        vmem((rows, 128), F32),
        vmem((crops, 128), F32),
        vmem((crops, 128), F32),
        vmem((ITERS, dp_count, lane_blocks, 128), F32),
        vmem((ITERS, nx, row_blocks + crop_blocks, 128), F32),
        vmem((ITERS, nz, row_blocks + crop_blocks, 128), F32),
        vmem((dp_count, 8, 128), F32),
        vmem((nx, 8, 128), F32),
        vmem((nz, 8, 128), F32),
        vmem((ny, CORES, 2, half, width), F32),
        vmem((ny, 2, half, width), F32),
        vmem((2, fy, 2, half, width), F32),
        vmem((ny, CORES, 2, half, width), F32),
        vmem((nx, nz, share, 128), F32),
        vmem((nz, nx, share, 128), F32),
        vmem((2, fx, 2, fz, share, 128), F32),
        vmem((2, fz, 2, share // 2, 128), F32),
        vmem((2, fz, 2, fx, share, 128), F32),
        vmem((2, fx, 2, share // 2, 128), F32),
        vmem((nx, nz, share, 128), F32),
        vmem((nz, nx, share, 128), F32),
        dma((ITERS, 2, dp_count)),
        dma((ITERS, 2, nx)),
        dma((ITERS, 2, nz)),
        dma((2, dp_count)),
        dma((2, nx)),
        dma((2, nz)),
        dma((2, ny)),
        dma((2, 2, fy, 2)),
        dma((2, 2, fx, 2)),
        dma((2, 2, fz, 2)),
        dma((2, 2, fz, 2)),
        dma((2, 2, fx, 2)),
        dma((2, 2, fy, 2)),
        dma((2, ny)),
        dma((2, 2, fz, 2)),
        dma((2, 2, fx, 2)),
        dma((2, 2, fx, 2)),
        dma((2, 2, fz, 2)),
        dma((CORES, ny)),
        dma((2, max(nx, nz))),
    ]
    in_vmem = pl.BlockSpec(memory_space=pltpu.VMEM)
    anywhere = pl.BlockSpec(memory_space=pl.ANY)
    grad_embed, grad_proto, loss = pl.pallas_call(
        functools.partial(kernel, sizes),
        out_shape=(
            jax.ShapeDtypeStruct((nx, nz, share, depth), F32),
            jax.ShapeDtypeStruct((2, half, cols), F32),
            jax.ShapeDtypeStruct((1, 1), F32),
        ),
        in_specs=[in_vmem] * 4,
        out_specs=(anywhere, anywhere, pl.BlockSpec(memory_space=pltpu.SMEM)),
        scratch_shapes=scratch,
        compiler_params=pltpu.CompilerParams(
            collective_id=0, has_side_effects=True, vmem_limit_bytes=60 * 1024 * 1024
        ),
    )(embeddings, queue, prototypes, pairing.reshape(1, crops))
    return (
        grad_embed.reshape(crops, depth),
        grad_proto.reshape(depth, cols),
        loss.reshape(()),
    )


def solution(mesh):
    nx = ALONG_X
    sizes = (mesh.shape["dp"] // CORES, nx, mesh.shape["proto"] // nx)
    return jax.shard_map(
        functools.partial(local, sizes),
        mesh=mesh,
        in_specs=(P("dp", None), P("dp", None), P(None, "proto"), P("dp")),
        out_specs=(P("dp", None), P(None, "proto"), P()),
        check_vma=False,
    )
```

```python
import functools
import math

import jax
import jax.numpy as jnp
from jax import lax
from jax.experimental import pallas as pl
from jax.experimental.pallas import tpu as pltpu
from jax.sharding import PartitionSpec as P

PROTOS = 65536
ITERS = 3
CORES = 2
ALONG_X = 4
LOG2E = math.log2(math.e)
F32 = jnp.float32
BF16 = jnp.bfloat16
MESH = pl.DeviceIdType.MESH


def inv_norm(sum_sq):
    shifted = sum_sq + 1e-06
    guess = lax.rsqrt(shifted)
    return guess * (1.5 - 0.5 * shifted * guess * guess)


def aligned(index, size):
    return pl.ds(pl.multiple_of(index * size, size), size)


def remote(src, dst, send_sem, recv_sem, device):
    return pltpu.make_async_remote_copy(
        src_ref=src,
        dst_ref=dst,
        send_sem=send_sem,
        recv_sem=recv_sem,
        device_id=device,
        device_id_type=MESH,
    )


def arrived(view, sems, device):
    remote(view, view, sems.at[0], sems.at[1], device).wait_recv()


def departed(view, sems, device):
    remote(view, view, sems.at[0], sems.at[1], device).wait_send()


def far_first(size):
    return sorted(range(1, size), key=lambda hop: (-min(hop, size - hop), hop))


class Exchange:
    def __init__(self, buf, sems, me, size, device):
        self.buf, self.sems, self.me, self.size, self.device = buf, sems, me, size, device

    def start(self, block):
        self.buf[self.me] = block
        for hop in far_first(self.size):
            slot = self.buf.at[self.me]
            peer = self.device(lax.rem(self.me + hop, self.size))
            remote(slot, slot, self.sems.at[0], self.sems.at[1], peer).start()

    def finish(self):
        others = self.buf.at[pl.ds(0, self.size - 1)]
        arrived(others, self.sems, self.device(self.me))
        departed(others, self.sems, self.device(self.me))
        total = self.buf[0]
        for slot in range(1, self.size):
            total = total + self.buf[slot]
        return total


class Scatter:
    def __init__(self, n, me, part, recv, sems, device):
        self.n, self.me, self.part, self.recv = n, me, part, recv
        self.sems, self.device = sems, device

    def start(self):
        for hop in far_first(self.n):
            piece = lax.rem(self.me + hop, self.n)
            remote(
                self.part(piece),
                self.recv.at[hop - 1],
                self.sems.at[0],
                self.sems.at[1],
                self.device(piece),
            ).start()

    def finish(self):
        arrived(self.recv, self.sems, self.device(self.me))
        total = self.part(self.me)[...]
        for hop in range(1, self.n):
            total = total + self.recv[hop - 1]
        return total

    def close(self):
        departed(self.recv, self.sems, self.device(self.me))


class Ring:
    def __init__(self, n, me, part, recv, sems, recv_sems, device):
        self.n, self.me, self.part, self.recv = n, me, part, recv
        self.sems, self.recv_sems, self.device = sems, recv_sems, device
        self.far = n // 2

    def at(self, hops):
        return lax.rem(self.me + hops + self.n, self.n)

    def copy(self, way, step, half, piece):
        return remote(
            self.part(piece, half),
            self.recv.at[way, step, half],
            self.sems.at[0],
            self.recv_sems.at[way, step],
            self.device(self.at(1 if way == 0 else -1)),
        )

    def add(self, way, step, half, piece):
        view = self.part(piece, half)
        view[...] = view[...] + self.recv[way, step, half]

    def first(self):
        for way in range(2):
            self.copy(way, 0, way, self.at(self.far)).start()

    def early(self, way):
        if self.far == 2:
            self.copy(way, 1, 1 - way, self.at(1 if way == 0 else -1)).start()

    def second(self):
        if self.far == 2:
            for way in range(2):
                piece = self.at(1 if way == 0 else -1)
                self.copy(way, 0, way, piece).wait_recv()
                self.add(way, 0, way, piece)
                self.copy(way, 1, way, piece).start()

    def finish(self):
        for way in range(2):
            if self.far == 2:
                view = self.recv.at[way, 1]
                remote(
                    view,
                    view,
                    self.sems.at[0],
                    self.recv_sems.at[way, 1],
                    self.device(self.me),
                ).wait_recv()
                self.add(way, 1, 0, self.me)
                self.add(way, 1, 1, self.me)
            else:
                self.copy(way, 0, way, self.me).wait_recv()
                self.add(way, 0, way, self.me)


def kernel(
    sizes,
    emb_hbm,
    que_hbm,
    pro_hbm,
    pair_hbm,
    out_e,
    out_p,
    out_l,
    emb,
    que,
    pro,
    pair,
    ex,
    sx,
    yx,
    rows_bf,
    part_bf,
    pro_bf,
    emb_t,
    pro_t,
    differ,
    colacc,
    lanes,
    softp,
    rbc,
    stb,
    qpart,
    dpbuf,
    xbuf,
    zbuf,
    ldp,
    lx,
    lz,
    pc,
    sib,
    yrecv,
    h1,
    h2,
    x1recv,
    z1recv,
    z2recv,
    x2recv,
    load_sems,
    dp_sems,
    x_sems,
    z_sems,
    loss_sems,
    sib_send,
    sib_recv,
    pair_sems,
    ring_sems,
    yg_recv,
    zg_recv,
    xg_recv,
):
    ny, nx, nz = sizes
    dp_count = ny * CORES
    crops, depth = emb.shape
    rows = crops + que.shape[0]
    cols = pro.shape[1]
    total_rows = rows * dp_count
    total_crops = crops * dp_count
    lane_blocks = cols // 128
    row_blocks = rows // 128
    crop_blocks = crops // 128
    width = cols // dp_count
    tile = 256

    my_dp = lax.axis_index("dp")
    my_proto = lax.axis_index("proto")
    my_y, my_c = my_dp // CORES, lax.rem(my_dp, CORES)
    my_z, my_x = my_proto // nx, lax.rem(my_proto, nx)

    def on_dp(index):
        return (index, my_proto)

    def on_x(index):
        return (my_dp, my_z * nx + index)

    def on_z(index):
        return (my_dp, index * nx + my_x)

    def on_y(index):
        return (index * CORES + my_c, my_proto)

    sibling = (my_y * CORES + 1 - my_c, my_proto)

    barrier = pltpu.get_barrier_semaphore()
    for me, size, device in ((my_z, nz, on_z), (my_x, nx, on_x), (my_dp, dp_count, on_dp)):
        for hop in far_first(size):
            pl.semaphore_signal(
                barrier, inc=1, device_id=device(lax.rem(me + hop, size)), device_id_type=MESH
            )

    loads = [
        pltpu.make_async_copy(source, target, load_sems.at[i])
        for i, (source, target) in enumerate(
            ((emb_hbm, emb), (que_hbm, que), (pro_hbm, pro), (pair_hbm, pair))
        )
    ]
    for load in loads:
        load.start()
    for load in loads:
        load.wait()

    @pl.loop(0, crops // tile)
    def _(i):
        block = aligned(i, tile)
        for source, first in ((emb, 0), (que, crops)):
            values = source[block, :].astype(F32)
            inv = inv_norm(jnp.sum(values * values, axis=1, keepdims=True))
            start = pl.multiple_of(first + i * tile, tile)
            rows_bf[pl.ds(start, tile), :] = (values * inv).astype(BF16)

    @pl.loop(0, cols // tile)
    def _(j):
        block = aligned(j, tile)
        values = pro[:, block].astype(F32)
        inv = inv_norm(jnp.sum(values * values, axis=0, keepdims=True))
        pro_bf[:, block] = (values * inv).astype(BF16)

    softp[...] = jnp.zeros_like(softp)

    @pl.loop(0, cols // tile)
    def _(j):
        block = aligned(j, tile)
        weights = pro_bf[:, block]
        acc = jnp.zeros((8, tile), F32)
        for i in range(rows // tile):
            lines = slice(i * tile, (i + 1) * tile)
            scores = jnp.dot(rows_bf[lines, :], weights, preferred_element_type=F32)
            if i < crops // tile:
                sx[lines, block] = scores
                soft = jnp.exp2(scores * (10.0 * LOG2E))
                folded = soft[:, :128]
                for k in range(1, tile // 128):
                    folded = folded + soft[:, k * 128 : (k + 1) * 128]
                softp[lines, :] += folded
                expo = soft * soft
            else:
                expo = jnp.exp2(scores * (20.0 * LOG2E))
            ex[lines, block] = expo
            acc = acc + jnp.sum(expo.reshape(tile // 8, 8, tile), axis=0)
        colacc[j] = acc

    def dense_cols():
        pieces = []
        for j in range(lane_blocks):
            k, part = j * 128 // tile, (j * 128) % tile
            pieces.append(jnp.sum(colacc[k, :, part : part + 128], axis=0, keepdims=True))
        return jnp.concatenate(pieces, axis=0)

    def dense_rows(source, blocks):
        pieces = []
        for b in range(blocks):
            pieces.append(
                jnp.sum(source[b * 128 : (b + 1) * 128, :].T, axis=0, keepdims=True)
            )
        return jnp.concatenate(pieces, axis=0)

    def spread_rows(target, dense, blocks):
        for b in range(blocks):
            target[b * 128 : (b + 1) * 128, :] = jnp.broadcast_to(
                dense[b : b + 1, :], (128, 128)
            ).T

    def col_pass():
        groups = 4

        def step(i, accs):
            accs = list(accs)
            for g in range(groups):
                lines = pl.ds(pl.multiple_of(i * 8 * groups + 8 * g, 8), 8)
                scale = rbc[lines, :]
                for j in range(lane_blocks):
                    accs[j] = accs[j] + ex[lines, j * 128 : (j + 1) * 128] * scale
            return tuple(accs)

        accs = lax.fori_loop(
            0, rows // (8 * groups), step, (jnp.zeros((8, 128), F32),) * lane_blocks
        )
        return jnp.concatenate([jnp.sum(a, axis=0, keepdims=True) for a in accs], axis=0)

    def spread_cols(dense):
        return [
            jnp.broadcast_to(dense[j : j + 1, :], (8, 128)) for j in range(lane_blocks)
        ]

    def row_pass(scales):
        groups = 4

        @pl.loop(0, rows // (8 * groups))
        def _(i):
            for g in range(groups):
                lines = pl.ds(pl.multiple_of(i * 8 * groups + 8 * g, 8), 8)
                acc = ex[lines, :128] * scales[0]
                for j in range(1, lane_blocks):
                    acc = acc + ex[lines, j * 128 : (j + 1) * 128] * scales[j]
                lanes[lines, :] = acc

    def partner_pass(scales):
        groups = 4

        @pl.loop(0, crops // (8 * groups))
        def _(i):
            for g in range(groups):
                lines = pl.ds(pl.multiple_of(i * 8 * groups + 8 * g, 8), 8)
                acc = jnp.zeros((8, 128), F32)
                for j in range(lane_blocks):
                    block = slice(j * 128, (j + 1) * 128)
                    code = yx[lines, block] * scales[j]
                    yx[lines, block] = code
                    acc = acc + code
                lanes[lines, :] = acc

    def soften(first, last):
        groups = 2

        @pl.loop(first // (8 * groups), last // (8 * groups))
        def _(i):
            for g in range(groups):
                lines = pl.ds(pl.multiple_of(i * 8 * groups + 8 * g, 8), 8)
                scale = stb[lines, :]
                acc = jnp.zeros((8, 128), F32)
                for j in range(lane_blocks):
                    block = slice(j * 128, (j + 1) * 128)
                    score = sx[lines, block]
                    acc = acc + yx[lines, block] * score
                    sx[lines, block] = jnp.exp2(score * (10.0 * LOG2E)) * scale
                qpart[lines, :] = acc

    def pick_partners():
        local_pair = pair[...] - my_dp * crops

        @pl.loop(0, crops // tile)
        def _(i):
            block = aligned(i, tile)
            line = lax.broadcasted_iota(jnp.int32, (tile, crops), 0) + i * tile
            pick = jnp.where(line == local_pair, 1.0, 0.0).astype(BF16)
            part_bf[block, :] = jnp.dot(
                pick, rows_bf[:crops, :], preferred_element_type=F32
            ).astype(BF16)

    def partner_exponents():
        @pl.loop(0, cols // tile)
        def _(j):
            block = aligned(j, tile)
            weights = pro_bf[:, block]
            for i in range(crops // tile):
                lines = slice(i * tile, (i + 1) * tile)
                scores = jnp.dot(part_bf[lines, :], weights, preferred_element_type=F32)
                soft = jnp.exp2(scores * (10.0 * LOG2E))
                yx[lines, block] = soft * soft

    def transposed_rows():
        @pl.loop(0, crops // tile)
        def _(i):
            block = aligned(i, tile)
            emb_t[:, block] = rows_bf[block, :].astype(F32).T.astype(BF16)

    def transposed_cols():
        @pl.loop(0, cols // tile)
        def _(j):
            block = aligned(j, tile)
            pro_t[block, :] = pro_bf[:, block].astype(F32).T.astype(BF16)

    pl.semaphore_wait(barrier, dp_count - 1 + nx - 1 + nz - 1)
    col_dense = dense_cols()
    soft_total = None
    row_sum = None
    for it in range(ITERS):
        over_dp = Exchange(dpbuf.at[it], dp_sems.at[it], my_dp, dp_count, on_dp)
        over_x = Exchange(xbuf.at[it], x_sems.at[it], my_x, nx, on_x)
        over_z = Exchange(zbuf.at[it], z_sems.at[it], my_z, nz, on_z)
        over_dp.start(col_dense)
        extra = jnp.zeros((crop_blocks, 128), F32)
        if it == 0:
            pick_partners()
            extra = dense_rows(softp, crop_blocks)
        elif it == 1:
            spread_rows(stb, 10.0 / soft_total, crop_blocks)
        elif it == 2:
            transposed_cols()
        col_scale = 1.0 / (PROTOS * over_dp.finish())
        if it < ITERS - 1:
            row_pass(spread_cols(col_scale))
            over_x.start(jnp.concatenate([dense_rows(lanes, row_blocks), extra], axis=0))
            if it == 0:
                transposed_rows()
            over_z.start(over_x.finish())
            if it == 0:
                partner_exponents()
            total = over_z.finish()
            if it == 0:
                soft_total = total[row_blocks:, :]
            spread_rows(rbc, 1.0 / (total_rows * total[:row_blocks, :]), row_blocks)
            col_dense = col_pass()
        else:
            partner_pass(spread_cols(10.0 * col_scale))
            filler = jnp.zeros((row_blocks, 128), F32)
            over_x.start(
                jnp.concatenate([dense_rows(lanes, crop_blocks), filler], axis=0)
            )
            soften(0, crops // 2)
            over_z.start(over_x.finish())
            soften(crops // 2, crops)
            row_sum = over_z.finish()[:crop_blocks, :]

    spread_rows(rbc, 10.0 / row_sum, crop_blocks)

    repeat = tile // 128
    for i in range(crops // tile):
        lines = slice(i * tile, (i + 1) * tile)
        scale = jnp.concatenate([rbc[lines, :]] * repeat, axis=1)

        @pl.loop(0, cols // tile)
        def _(j):
            block = aligned(j, tile)
            value = sx[lines, block] - yx[lines, block] * scale
            differ[lines, block] = value.astype(BF16)

    share = crops // (nx * nz)
    first_share = share - share // 4
    x_line = nz * share

    x1 = Ring(
        nx,
        my_x,
        lambda t, half: h1.at[t, pl.ds(half * (nz // 2), nz // 2)],
        x1recv,
        ring_sems.at[0],
        pair_sems.at[0],
        on_x,
    )
    z1 = Scatter(nz, my_z, lambda t: h1.at[my_x, t], z1recv, ring_sems.at[1], on_z)
    z2 = Scatter(nz, my_z, lambda t: h2.at[t], z2recv, ring_sems.at[2], on_z)
    x2 = Scatter(nx, my_x, lambda t: h2.at[my_z, t], x2recv, ring_sems.at[3], on_x)
    for hops in [nx // 2] + ([1, -1] if nx == 4 else []) + [0]:
        t = x1.at(hops)
        lines = aligned(t, x_line)
        cot = jnp.dot(differ[lines, :], pro_t[...], preferred_element_type=F32)
        for pz in range(nz):
            h1[t, pz] = cot[pz * share : pz * share + first_share, :]
            h2[pz, t] = cot[pz * share + first_share : (pz + 1) * share, :]
        if hops == nx // 2:
            x1.first()
        elif hops == 1:
            x1.early(0)
        elif hops == -1:
            x1.early(1)
    z2.start()

    half_depth = depth // 2

    def piece(t, core):
        block = aligned(t * CORES + core, width)
        cot = jnp.dot(emb_t[...], differ[:, block], preferred_element_type=F32)
        pc[t, core, 0] = cot[:half_depth, :]
        pc[t, core, 1] = cot[half_depth:, :]

    def to_sibling(number, t):
        return remote(
            pc.at[t, 1 - my_c], sib.at[number], sib_send.at[0], sib_recv.at[number], sibling
        )

    y_ring = Ring(
        ny,
        my_y,
        lambda t, half: pc.at[t, my_c, half],
        yrecv,
        ring_sems.at[4],
        pair_sems.at[1],
        on_y,
    )
    near = [1, -1] if ny == 4 else []
    order = [ny // 2] + near + [0]
    for number, hops in enumerate(order):
        t = y_ring.at(hops)
        piece(t, 1 - my_c)
        to_sibling(number, t).start()
        piece(t, my_c)
        to_sibling(number, t).wait_recv()
        pc[t, my_c] = pc[t, my_c] + sib[number]
        if hops == ny // 2:
            y_ring.first()
        elif hops == 1:
            y_ring.early(0)
        elif hops == -1:
            y_ring.early(1)

    def add_up(i, acc):
        lines = aligned(i, 8)
        return acc + qpart[lines, :] * rbc[lines, :]

    code_score = lax.fori_loop(0, crops // 8, add_up, jnp.zeros((8, 128), F32))
    log_total = jnp.log(soft_total) * (1.0 / (nx * nz))
    if crop_blocks != 8:
        log_total = jnp.broadcast_to(jnp.sum(log_total, axis=0, keepdims=True), (8, 128)) / 8.0
    loss_dp = Exchange(ldp, loss_sems.at[0], my_dp, dp_count, on_dp)
    loss_x = Exchange(lx, loss_sems.at[1], my_x, nx, on_x)
    loss_z = Exchange(lz, loss_sems.at[2], my_z, nz, on_z)
    loss_dp.start(log_total - code_score)

    x1.second()
    y_ring.second()
    loss_x.start(loss_dp.finish())
    h2[my_z] = z2.finish()
    x2.start()
    x1.finish()
    z1.start()
    loss_z.start(loss_x.finish())
    y_ring.finish()

    def columns(t, core):
        return aligned(t * CORES + core, width)

    block = columns(my_y, my_c)
    values = pro[:, block].astype(F32)
    inv = inv_norm(jnp.sum(values * values, axis=0, keepdims=True))
    cots = [pc[my_y, my_c, 0], pc[my_y, my_c, 1]]
    along = jnp.sum(cots[0] * values[:half_depth, :], axis=0, keepdims=True) + jnp.sum(
        cots[1] * values[half_depth:, :], axis=0, keepdims=True
    )
    factor = PROTOS / math.sqrt(total_crops)
    pull = along * (inv * inv * inv) * factor
    scale = inv * factor
    out_p[0, :, block] = cots[0] * scale - values[:half_depth, :] * pull
    out_p[1, :, block] = cots[1] * scale - values[half_depth:, :] * pull

    def along_y(way, step, half, t):
        view = out_p.at[half, :, columns(t, my_c)]
        peer = on_y(y_ring.at(1 if way == 0 else -1))
        return remote(view, view, ring_sems.at[5, 0], yg_recv.at[way, step, half], peer)

    def hand_on(t):
        view = out_p.at[:, :, columns(t, my_c)]
        remote(view, view, ring_sems.at[6, 0], ring_sems.at[6, 1], sibling).start()

    if ny == 4:
        for part in range(2):
            along_y(0, 0, part, my_y).start()
            along_y(1, 0, 1 - part, my_y).start()
    else:
        along_y(0, 1, 0, my_y).start()
        along_y(1, 1, 1, my_y).start()
    hand_on(my_y)

    def pull_rows(cot, first, count):
        values = emb[aligned(my_x * nz + my_z, share), :].astype(F32)
        values = values[first : first + count, :]
        inv = inv_norm(jnp.sum(values * values, axis=1, keepdims=True))
        along = jnp.sum(cot * values, axis=1, keepdims=True)
        factor = math.sqrt(PROTOS)
        out_e[my_x, my_z, pl.ds(first, count)] = cot * (inv * factor) - values * (
            along * (inv * inv * inv) * factor
        )

    rest = share - first_share
    late = pl.ds(first_share, rest)
    soon = pl.ds(0, first_share)

    pull_rows(x2.finish(), first_share, rest)
    for hop in far_first(nx):
        view = out_e.at[my_x, my_z, late]
        remote(
            view, view, ring_sems.at[7, 0], ring_sems.at[7, 1], on_x(x1.at(hop))
        ).start()
    loss_total = loss_z.finish()

    pull_rows(z1.finish(), 0, first_share)

    def z_at(hops):
        return lax.rem(my_z + hops + nz, nz)

    def near_x(way, rel):
        view = out_e.at[my_x, z_at(rel), soon]
        peer = on_x(x1.at(1 if way == 0 else -1))
        return remote(view, view, ring_sems.at[9, 0], xg_recv.at[way, rel], peer)

    def from_x(way, rel):
        view = out_e.at[x1.at(-1 if way == 0 else 1), z_at(rel), soon]
        peer = on_x(x1.at(1 if way == 0 else -1))
        return remote(view, view, ring_sems.at[10, 0], ring_sems.at[10, 1], peer)

    def over_z_at(rel):
        view = out_e.at[my_x, my_z, soon]
        return remote(view, view, ring_sems.at[8, 0], zg_recv.at[rel], on_z(z_at(rel)))

    for hop in sorted(range(1, nz), key=lambda h: (min(h, nz - h), h)):
        over_z_at(hop).start()
    near_x(0, 0).start()
    near_x(1, 0).start()

    pending = sorted(range(nz), key=lambda h: (min(h, nz - h), h))
    ahead = [r for r in pending if 1 <= r <= nz // 2]

    def receive_z(rel):
        view = out_e.at[my_x, z_at(nz - rel), soon]
        remote(view, view, ring_sems.at[8, 0], zg_recv.at[rel], on_z(my_z)).wait_recv()
        near_x(0, nz - rel).start()
        near_x(1, nz - rel).start()

    def take_y(way):
        t = y_ring.at(-1 if way == 0 else 1)
        for part in (way, 1 - way):
            view = out_p.at[part, :, columns(t, my_c)]
            remote(
                view, view, ring_sems.at[5, 0], yg_recv.at[way, 0, part], on_y(my_y)
            ).wait_recv()
            if part == way:
                along_y(way, 1, part, t).start()
        hand_on(t)

    def send_late():
        arrived(out_e.at[pl.ds(0, nx - 1), 0, late], ring_sems.at[7], on_x(my_x))
        for hop in far_first(nz):
            view = out_e.at[:, my_z, late]
            remote(
                view, view, ring_sems.at[11, 0], ring_sems.at[11, 1], on_z(z_at(hop))
            ).start()

    steps = [lambda r=r: receive_z(r) for r in pending[1:]]
    steps.insert(min(2, len(steps)), send_late)
    if ny == 4:
        steps.insert(min(4, len(steps)), lambda: take_y(0))
        steps.insert(min(5, len(steps)), lambda: take_y(1))
    for step in steps:
        step()
    if nx == 4:
        for rel in pending:
            for way in range(2):
                view = out_e.at[x1.at(-1 if way == 0 else 1), z_at(rel), soon]
                remote(
                    view, view, ring_sems.at[9, 0], xg_recv.at[way, rel], on_x(my_x)
                ).wait_recv()
                if (rel in ahead) == (way == 0):
                    from_x(way, rel).start()
    else:
        for rel in pending:
            for way in range(2):
                view = out_e.at[x1.at(-1 if way == 0 else 1), z_at(rel), soon]
                remote(
                    view, view, ring_sems.at[9, 0], xg_recv.at[way, rel], on_x(my_x)
                ).wait_recv()

    far_y = y_ring.at(ny // 2)
    for way in range(2):
        view = out_p.at[way, :, columns(far_y, my_c)]
        remote(
            view, view, ring_sems.at[5, 0], yg_recv.at[way, 1, way], on_y(my_y)
        ).wait_recv()
    hand_on(far_y)
    out_l[0, 0] = jnp.sum(loss_total) / total_crops

    arrived(out_e.at[:, pl.ds(0, nz - 1), late], ring_sems.at[11], on_z(my_z))
    if nx == 4:
        arrived(out_e.at[0, :, soon], ring_sems.at[10], on_x(my_x))
    own = out_p.at[:, :, pl.ds(0, ny * width)]
    arrived(own, ring_sems.at[6], sibling)
    departed(own, ring_sems.at[6], sibling)
    departed(h1.at[pl.ds(0, nx - 1)], ring_sems.at[0], on_x(my_x))
    for ring in (z1, z2, x2):
        ring.close()
    departed(pc.at[pl.ds(0, ny - 1), 0], ring_sems.at[4], on_y(my_y))
    remote(pc.at[:, 0], pc.at[:, 0], sib_send.at[0], sib_recv.at[0], sibling).wait_send()
    departed(out_p.at[:, :, pl.ds(0, (ny - 1) * width)], ring_sems.at[5], on_y(my_y))
    departed(out_e.at[pl.ds(0, nx - 1), 0, late], ring_sems.at[7], on_x(my_x))
    departed(out_e.at[0, pl.ds(0, nz - 1), soon], ring_sems.at[8], on_z(my_z))
    departed(out_e.at[pl.ds(0, 2), :, soon], ring_sems.at[9], on_x(my_x))
    if nx == 4:
        departed(out_e.at[0, :, soon], ring_sems.at[10], on_x(my_x))
    departed(out_e.at[:, pl.ds(0, nz - 1), late], ring_sems.at[11], on_z(my_z))


def local(sizes, embeddings, queue, prototypes, pairing):
    ny, nx, nz = sizes
    dp_count = ny * CORES
    crops, depth = embeddings.shape
    rows = crops + queue.shape[0]
    cols = prototypes.shape[1]
    width = cols // dp_count
    share = crops // (nx * nz)
    first_share = share - share // 4
    rest = share // 4
    row_blocks, crop_blocks, lane_blocks = rows // 128, crops // 128, cols // 128
    half = depth // 2
    tile = 256
    dma = pltpu.SemaphoreType.DMA
    vmem = pltpu.VMEM
    scratch = [
        vmem((crops, depth), BF16),
        vmem((rows - crops, depth), BF16),
        vmem((depth, cols), BF16),
        vmem((1, crops), jnp.int32),
        vmem((rows, cols), F32),
        vmem((crops, cols), F32),
        vmem((crops, cols), F32),
        vmem((rows, depth), BF16),
        vmem((crops, depth), BF16),
        vmem((depth, cols), BF16),
        vmem((depth, crops), BF16),
        vmem((cols, depth), BF16),
        vmem((crops, cols), BF16),
        vmem((cols // tile, 8, tile), F32),
        vmem((rows, 128), F32),
        vmem((crops, 128), F32),
        vmem((rows, 128), F32),
        vmem((crops, 128), F32),
        vmem((crops, 128), F32),
        vmem((ITERS, dp_count, lane_blocks, 128), F32),
        vmem((ITERS, nx, row_blocks + crop_blocks, 128), F32),
        vmem((ITERS, nz, row_blocks + crop_blocks, 128), F32),
        vmem((dp_count, 8, 128), F32),
        vmem((nx, 8, 128), F32),
        vmem((nz, 8, 128), F32),
        vmem((ny, CORES, 2, half, width), F32),
        vmem((ny, 2, half, width), F32),
        vmem((2, 2, 2, half, width), F32),
        vmem((nx, nz, first_share, depth), F32),
        vmem((nz, nx, rest, depth), F32),
        vmem((2, 2, 2, nz // 2, first_share, depth), F32),
        vmem((nz - 1, first_share, depth), F32),
        vmem((nz - 1, nx, rest, depth), F32),
        vmem((nx - 1, rest, depth), F32),
        dma((4,)),
        dma((ITERS, 2)),
        dma((ITERS, 2)),
        dma((ITERS, 2)),
        dma((3, 2)),
        dma((1,)),
        dma((ny,)),
        dma((2, 2, 2)),
        dma((12, 2)),
        dma((2, 2, 2)),
        dma((nz,)),
        dma((2, nz)),
    ]
    in_vmem = pl.BlockSpec(memory_space=pltpu.VMEM)
    anywhere = pl.BlockSpec(memory_space=pl.ANY)
    grad_embed, grad_proto, loss = pl.pallas_call(
        functools.partial(kernel, sizes),
        out_shape=(
            pltpu.VMEM((nx, nz, share, depth), F32),
            pltpu.VMEM((2, half, cols), F32),
            jax.ShapeDtypeStruct((1, 1), F32),
        ),
        in_specs=[anywhere] * 4,
        out_specs=(in_vmem, in_vmem, pl.BlockSpec(memory_space=pltpu.SMEM)),
        scratch_shapes=scratch,
        compiler_params=pltpu.CompilerParams(
            collective_id=0, has_side_effects=True, vmem_limit_bytes=59 * 1024 * 1024
        ),
    )(embeddings, queue, prototypes, pairing.reshape(1, crops))
    return (
        grad_embed.reshape(crops, depth),
        grad_proto.reshape(depth, cols),
        loss.reshape(()),
    )


def solution(mesh):
    nx = ALONG_X
    sizes = (mesh.shape["dp"] // CORES, nx, mesh.shape["proto"] // nx)
    return jax.shard_map(
        functools.partial(local, sizes),
        mesh=mesh,
        in_specs=(P("dp", None), P("dp", None), P(None, "proto"), P("dp")),
        out_specs=(P("dp", None), P(None, "proto"), P()),
        check_vma=False,
    )
```

```python
import functools
import math

import jax
import jax.numpy as jnp
from jax import lax
from jax.experimental import pallas as pl
from jax.experimental.pallas import tpu as pltpu
from jax.sharding import PartitionSpec as P

PROTOS = 65536
ITERS = 3
CORES = 2
ALONG_X = 4
LOG2E = math.log2(math.e)
F32 = jnp.float32
BF16 = jnp.bfloat16
MESH = pl.DeviceIdType.MESH


def inv_norm(sum_sq):
    shifted = sum_sq + 1e-06
    guess = lax.rsqrt(shifted)
    return guess * (1.5 - 0.5 * shifted * guess * guess)


def aligned(index, size):
    return pl.ds(pl.multiple_of(index * size, size), size)


def remote(src, dst, send_sem, recv_sem, device):
    return pltpu.make_async_remote_copy(
        src_ref=src,
        dst_ref=dst,
        send_sem=send_sem,
        recv_sem=recv_sem,
        device_id=device,
        device_id_type=MESH,
    )


def arrived(view, sems, device):
    remote(view, view, sems.at[0], sems.at[1], device).wait_recv()


def departed(view, sems, device):
    remote(view, view, sems.at[0], sems.at[1], device).wait_send()


def far_first(size):
    return sorted(range(1, size), key=lambda hop: (-min(hop, size - hop), hop))


class Exchange:
    def __init__(self, buf, sems, me, size, device):
        self.buf, self.sems, self.me, self.size, self.device = buf, sems, me, size, device

    def start(self, block):
        self.buf[self.me] = block
        for hop in far_first(self.size):
            slot = self.buf.at[self.me]
            peer = self.device(lax.rem(self.me + hop, self.size))
            remote(slot, slot, self.sems.at[0], self.sems.at[1], peer).start()

    def finish(self):
        others = self.buf.at[pl.ds(0, self.size - 1)]
        arrived(others, self.sems, self.device(self.me))
        departed(others, self.sems, self.device(self.me))
        total = self.buf[0]
        for slot in range(1, self.size):
            total = total + self.buf[slot]
        return total


class Scatter:
    def __init__(self, n, me, part, recv, sems, device):
        self.n, self.me, self.part, self.recv = n, me, part, recv
        self.sems, self.device = sems, device

    def start(self):
        for hop in far_first(self.n):
            piece = lax.rem(self.me + hop, self.n)
            remote(
                self.part(piece),
                self.recv.at[hop - 1],
                self.sems.at[0],
                self.sems.at[1],
                self.device(piece),
            ).start()

    def finish(self):
        arrived(self.recv, self.sems, self.device(self.me))
        total = self.part(self.me)[...]
        for hop in range(1, self.n):
            total = total + self.recv[hop - 1]
        return total

    def close(self):
        departed(self.recv, self.sems, self.device(self.me))


class Ring:
    def __init__(self, n, me, part, recv, sems, recv_sems, device):
        self.n, self.me, self.part, self.recv = n, me, part, recv
        self.sems, self.recv_sems, self.device = sems, recv_sems, device
        self.far = n // 2

    def at(self, hops):
        return lax.rem(self.me + hops + self.n, self.n)

    def copy(self, way, step, half, piece):
        return remote(
            self.part(piece, half),
            self.recv.at[way, step, half],
            self.sems.at[0],
            self.recv_sems.at[way, step],
            self.device(self.at(1 if way == 0 else -1)),
        )

    def add(self, way, step, half, piece):
        view = self.part(piece, half)
        view[...] = view[...] + self.recv[way, step, half]

    def first(self):
        for way in range(2):
            self.copy(way, 0, way, self.at(self.far)).start()

    def early(self, way):
        if self.far == 2:
            self.copy(way, 1, 1 - way, self.at(1 if way == 0 else -1)).start()

    def second(self):
        if self.far == 2:
            for way in range(2):
                piece = self.at(1 if way == 0 else -1)
                self.copy(way, 0, way, piece).wait_recv()
                self.add(way, 0, way, piece)
                self.copy(way, 1, way, piece).start()

    def finish(self):
        for way in range(2):
            if self.far == 2:
                view = self.recv.at[way, 1]
                remote(
                    view,
                    view,
                    self.sems.at[0],
                    self.recv_sems.at[way, 1],
                    self.device(self.me),
                ).wait_recv()
                self.add(way, 1, 0, self.me)
                self.add(way, 1, 1, self.me)
            else:
                self.copy(way, 0, way, self.me).wait_recv()
                self.add(way, 0, way, self.me)


def kernel(
    sizes,
    emb_hbm,
    que_hbm,
    pro_hbm,
    pair_hbm,
    out_e,
    out_p,
    out_l,
    emb,
    que,
    pro,
    pair,
    ex,
    sx,
    yx,
    rows_bf,
    part_bf,
    pro_bf,
    emb_t,
    pro_t,
    differ,
    colacc,
    dense,
    softp,
    rbc,
    stb,
    qpart,
    dpbuf,
    xbuf,
    zbuf,
    sxbuf,
    szbuf,
    ldp,
    lx,
    lz,
    pc,
    sib,
    yrecv,
    h1,
    h2,
    x1recv,
    z1recv,
    z2recv,
    x2recv,
    load_sems,
    dp_sems,
    x_sems,
    z_sems,
    soft_sems,
    loss_sems,
    sib_send,
    sib_recv,
    y_sems,
    y_pairs,
    ring_sems,
    x1_sems,
    x1_pairs,
    z1_sems,
    yg_recv,
    zg_recv,
):
    ny, nx, nz = sizes
    dp_count = ny * CORES
    crops, depth = emb.shape
    rows = crops + que.shape[0]
    cols = pro.shape[1]
    total_rows = rows * dp_count
    total_crops = crops * dp_count
    lane_blocks = cols // 128
    row_blocks = rows // 128
    crop_blocks = crops // 128
    width = cols // dp_count
    tile = 256

    my_dp = lax.axis_index("dp")
    my_proto = lax.axis_index("proto")
    my_y, my_c = my_dp // CORES, lax.rem(my_dp, CORES)
    my_z, my_x = my_proto // nx, lax.rem(my_proto, nx)

    def on_dp(index):
        return (index, my_proto)

    def on_x(index):
        return (my_dp, my_z * nx + index)

    def on_z(index):
        return (my_dp, index * nx + my_x)

    def on_y(index):
        return (index * CORES + my_c, my_proto)

    sibling = (my_y * CORES + 1 - my_c, my_proto)

    barrier = pltpu.get_barrier_semaphore()
    for me, size, device in ((my_z, nz, on_z), (my_x, nx, on_x), (my_dp, dp_count, on_dp)):
        for hop in far_first(size):
            pl.semaphore_signal(
                barrier, inc=1, device_id=device(lax.rem(me + hop, size)), device_id_type=MESH
            )

    loads = [
        pltpu.make_async_copy(source, target, load_sems.at[i])
        for i, (source, target) in enumerate(
            ((emb_hbm, emb), (que_hbm, que), (pro_hbm, pro), (pair_hbm, pair))
        )
    ]
    for load in loads:
        load.start()
    loads[0].wait()
    loads[1].wait()

    @pl.loop(0, crops // tile)
    def _(i):
        block = aligned(i, tile)
        for source, first in ((emb, 0), (que, crops)):
            values = source[block, :].astype(F32)
            inv = inv_norm(jnp.sum(values * values, axis=1, keepdims=True))
            start = pl.multiple_of(first + i * tile, tile)
            rows_bf[pl.ds(start, tile), :] = (values * inv).astype(BF16)

    loads[2].wait()
    loads[3].wait()

    @pl.loop(0, cols // tile)
    def _(j):
        block = aligned(j, tile)
        values = pro[:, block].astype(F32)
        inv = inv_norm(jnp.sum(values * values, axis=0, keepdims=True))
        pro_bf[:, block] = (values * inv).astype(BF16)

    softp[...] = jnp.zeros_like(softp)

    @pl.loop(0, cols // tile)
    def _(j):
        block = aligned(j, tile)
        weights = pro_bf[:, block]
        acc = jnp.zeros((8, tile), F32)
        for i in range(rows // tile):
            lines = slice(i * tile, (i + 1) * tile)
            scores = jnp.dot(rows_bf[lines, :], weights, preferred_element_type=F32)
            if i < crops // tile:
                sx[lines, block] = scores
                soft = jnp.exp2(scores * (10.0 * LOG2E))
                folded = soft[:, :128]
                for k in range(1, tile // 128):
                    folded = folded + soft[:, k * 128 : (k + 1) * 128]
                softp[lines, :] += folded
                expo = soft * soft
            else:
                expo = jnp.exp2(scores * (20.0 * LOG2E))
            ex[lines, block] = expo
            acc = acc + jnp.sum(expo.reshape(tile // 8, 8, tile), axis=0)
        colacc[j] = acc

    def dense_cols():
        pieces = []
        for j in range(lane_blocks):
            k, part = j * 128 // tile, (j * 128) % tile
            pieces.append(jnp.sum(colacc[k, :, part : part + 128], axis=0, keepdims=True))
        return jnp.concatenate(pieces, axis=0)

    def dense_rows(source, blocks):
        pieces = []
        for b in range(blocks):
            pieces.append(
                jnp.sum(source[b * 128 : (b + 1) * 128, :].T, axis=0, keepdims=True)
            )
        return jnp.concatenate(pieces, axis=0)

    def spread_rows(target, dense, blocks):
        for b in range(blocks):
            target[b * 128 : (b + 1) * 128, :] = jnp.broadcast_to(
                dense[b : b + 1, :], (128, 128)
            ).T

    def col_pass():
        groups = 4

        def step(i, accs):
            accs = list(accs)
            for g in range(groups):
                lines = pl.ds(pl.multiple_of(i * 8 * groups + 8 * g, 8), 8)
                scale = rbc[lines, :]
                for j in range(lane_blocks):
                    accs[j] = accs[j] + ex[lines, j * 128 : (j + 1) * 128] * scale
            return tuple(accs)

        accs = lax.fori_loop(
            0, rows // (8 * groups), step, (jnp.zeros((8, 128), F32),) * lane_blocks
        )
        return jnp.concatenate([jnp.sum(a, axis=0, keepdims=True) for a in accs], axis=0)

    def spread_cols(dense):
        return [
            jnp.broadcast_to(dense[j : j + 1, :], (8, 128)) for j in range(lane_blocks)
        ]

    def row_sums(target, count, line_sums):
        pair = 2

        @pl.loop(0, count // (128 * pair))
        def _(i):
            for k in range(pair):
                first = (i * pair + k) * 128
                accs = [
                    line_sums(pl.ds(pl.multiple_of(first + 8 * g, 8), 8)) for g in range(16)
                ]
                turned = jnp.concatenate(accs, axis=0).T
                target[pl.ds(i * pair + k, 1), :] = jnp.sum(turned, axis=0, keepdims=True)

    def row_pass(scales):
        def line_sums(lines):
            acc = ex[lines, :128] * scales[0]
            for j in range(1, lane_blocks):
                acc = acc + ex[lines, j * 128 : (j + 1) * 128] * scales[j]
            return acc

        row_sums(dense, rows, line_sums)

    def partner_pass(scales):
        def line_sums(lines):
            acc = jnp.zeros((8, 128), F32)
            for j in range(lane_blocks):
                block = slice(j * 128, (j + 1) * 128)
                code = yx[lines, block] * scales[j]
                yx[lines, block] = code
                acc = acc + code
            return acc

        row_sums(dense, crops, line_sums)

    def soften(first, last):
        groups = 2

        @pl.loop(first // (8 * groups), last // (8 * groups))
        def _(i):
            for g in range(groups):
                lines = pl.ds(pl.multiple_of(i * 8 * groups + 8 * g, 8), 8)
                scale = stb[lines, :]
                acc = jnp.zeros((8, 128), F32)
                for j in range(lane_blocks):
                    block = slice(j * 128, (j + 1) * 128)
                    score = sx[lines, block]
                    acc = acc + yx[lines, block] * score
                    sx[lines, block] = jnp.exp2(score * (10.0 * LOG2E)) * scale
                qpart[lines, :] = acc

    def pick_partners():
        local_pair = pair[...] - my_dp * crops

        @pl.loop(0, crops // tile)
        def _(i):
            block = aligned(i, tile)
            line = lax.broadcasted_iota(jnp.int32, (tile, crops), 0) + i * tile
            pick = jnp.where(line == local_pair, 1.0, 0.0).astype(BF16)
            part_bf[block, :] = jnp.dot(
                pick, rows_bf[:crops, :], preferred_element_type=F32
            ).astype(BF16)

    def partner_exponents():
        @pl.loop(0, cols // tile)
        def _(j):
            block = aligned(j, tile)
            weights = pro_bf[:, block]
            for i in range(crops // tile):
                lines = slice(i * tile, (i + 1) * tile)
                scores = jnp.dot(part_bf[lines, :], weights, preferred_element_type=F32)
                soft = jnp.exp2(scores * (10.0 * LOG2E))
                yx[lines, block] = soft * soft

    def transposed_rows():
        @pl.loop(0, crops // tile)
        def _(i):
            block = aligned(i, tile)
            emb_t[:, block] = rows_bf[block, :].astype(F32).T.astype(BF16)

    def transposed_cols():
        @pl.loop(0, cols // tile)
        def _(j):
            block = aligned(j, tile)
            pro_t[block, :] = pro_bf[:, block].astype(F32).T.astype(BF16)

    pl.semaphore_wait(barrier, dp_count - 1 + nx - 1 + nz - 1)
    col_dense = dense_cols()
    soft_total = None
    row_sum = None
    soft_x = Exchange(sxbuf, soft_sems.at[0], my_x, nx, on_x)
    soft_z = Exchange(szbuf, soft_sems.at[1], my_z, nz, on_z)
    for it in range(ITERS):
        blocks = pl.ds(0, row_blocks if it < ITERS - 1 else crop_blocks)
        over_dp = Exchange(dpbuf.at[it], dp_sems.at[it], my_dp, dp_count, on_dp)
        over_x = Exchange(xbuf.at[it, :, blocks], x_sems.at[it], my_x, nx, on_x)
        over_z = Exchange(zbuf.at[it, :, blocks], z_sems.at[it], my_z, nz, on_z)
        over_dp.start(col_dense)
        if it == 0:
            pick_partners()
            soft_part = dense_rows(softp, crop_blocks)
        elif it == 1:
            soft_x.start(soft_part)
            transposed_cols()
        else:
            soft_total = soft_z.finish()
            spread_rows(stb, 10.0 / soft_total, crop_blocks)
        col_scale = 1.0 / (PROTOS * over_dp.finish())
        if it < ITERS - 1:
            row_pass(spread_cols(col_scale))
            over_x.start(dense[...])
            if it == 0:
                transposed_rows()
            else:
                soft_z.start(soft_x.finish())
            over_z.start(over_x.finish())
            if it == 0:
                partner_exponents()
            total = over_z.finish()
            spread_rows(rbc, 1.0 / (total_rows * total), row_blocks)
            col_dense = col_pass()
        else:
            partner_pass(spread_cols(10.0 * col_scale))
            over_x.start(dense[:crop_blocks, :])
            soften(0, crops // 2)
            over_z.start(over_x.finish())
            soften(crops // 2, crops)
            row_sum = over_z.finish()

    spread_rows(rbc, 10.0 / row_sum, crop_blocks)

    share = crops // (nx * nz)
    rest = share // 4
    groups = 3
    first_share = groups * rest
    x_line = nz * share

    def x_ring(g):
        return Ring(
            nx,
            my_x,
            lambda t, half: h1.at[g, t, pl.ds(half * (nz // 2), nz // 2)],
            x1recv.at[g],
            x1_sems.at[g],
            x1_pairs.at[g],
            on_x,
        )

    def z_scatter(g):
        return Scatter(nz, my_z, lambda t: h1.at[g, my_x, t], z1recv.at[g], z1_sems.at[g], on_z)

    x1 = [x_ring(g) for g in range(groups)]
    z1 = [z_scatter(g) for g in range(groups)]
    z2 = Scatter(nz, my_z, lambda t: h2.at[t], z2recv, ring_sems.at[2], on_z)
    x2 = Scatter(nx, my_x, lambda t: h2.at[my_z, t], x2recv, ring_sems.at[3], on_x)

    repeat = tile // 128
    for hops in [nx // 2] + ([1, -1] if nx == 4 else []) + [0]:
        t = x1[0].at(hops)
        lines = aligned(t, x_line)
        scale = jnp.concatenate([rbc[lines, :]] * repeat, axis=1)
        for j in range(cols // tile):
            block = slice(j * tile, (j + 1) * tile)
            value = sx[lines, block] - yx[lines, block] * scale
            differ[lines, block] = value.astype(BF16)
        cot = jnp.dot(differ[lines, :], pro_t[...], preferred_element_type=F32)
        for pz in range(nz):
            for g in range(groups):
                first = pz * share + g * rest
                h1[g, t, pz] = cot[first : first + rest, :]
            h2[pz, t] = cot[pz * share + first_share : (pz + 1) * share, :]
        for ring in x1:
            if hops == nx // 2:
                ring.first()
            elif hops == 1:
                ring.early(0)
            elif hops == -1:
                ring.early(1)
    z2.start()

    half_depth = depth // 2
    parts = 2
    narrow = width // parts

    def piece(t, core):
        block = aligned(t * CORES + core, width)
        cot = jnp.dot(emb_t[...], differ[:, block], preferred_element_type=F32)
        for part in range(parts):
            across = slice(part * narrow, (part + 1) * narrow)
            pc[part, t, core, 0] = cot[:half_depth, across]
            pc[part, t, core, 1] = cot[half_depth:, across]

    def to_sibling(number, t):
        return remote(
            pc.at[:, t, 1 - my_c], sib.at[number], sib_send.at[0], sib_recv.at[number], sibling
        )

    def y_ring_of(part):
        return Ring(
            ny,
            my_y,
            lambda t, half: pc.at[part, t, my_c, half],
            yrecv.at[part],
            y_sems.at[part],
            y_pairs.at[part],
            on_y,
        )

    y_rings = [y_ring_of(part) for part in range(parts)]
    y_at = y_rings[0].at
    near = [1, -1] if ny == 4 else []
    order = [ny // 2] + near + [0]
    for number, hops in enumerate(order):
        t = y_at(hops)
        piece(t, 1 - my_c)
        to_sibling(number, t).start()
        piece(t, my_c)
        to_sibling(number, t).wait_recv()
        for part in range(parts):
            pc[part, t, my_c] = pc[part, t, my_c] + sib[number, part]
        if hops == ny // 2:
            y_rings[0].first()
        elif hops == 1:
            y_rings[0].early(0)
        elif hops == -1:
            y_rings[0].early(1)
    y_rings[1].first()

    def add_up(i, acc):
        lines = aligned(i, 8)
        return acc + qpart[lines, :] * rbc[lines, :]

    code_score = lax.fori_loop(0, crops // 8, add_up, jnp.zeros((8, 128), F32))
    log_total = jnp.log(soft_total) * (1.0 / (nx * nz))
    if crop_blocks != 8:
        log_total = jnp.broadcast_to(jnp.sum(log_total, axis=0, keepdims=True), (8, 128)) / 8.0
    loss_dp = Exchange(ldp, loss_sems.at[0], my_dp, dp_count, on_dp)
    loss_x = Exchange(lx, loss_sems.at[1], my_x, nx, on_x)
    loss_z = Exchange(lz, loss_sems.at[2], my_z, nz, on_z)
    loss_dp.start(log_total - code_score)

    for ring in x1:
        ring.second()
    y_rings[0].second()
    y_rings[1].early(0)
    y_rings[1].early(1)
    for ring, scatter in zip(x1, z1):
        ring.finish()
        scatter.start()
    y_rings[1].second()
    h2[my_z] = z2.finish()
    x2.start()
    loss_x.start(loss_dp.finish())

    def columns(t, core, part):
        first = (t * CORES + core) * width + part * narrow
        return pl.ds(pl.multiple_of(first, narrow), narrow)

    def pull_columns(part):
        block = columns(my_y, my_c, part)
        values = pro[:, block].astype(F32)
        inv = inv_norm(jnp.sum(values * values, axis=0, keepdims=True))
        cots = [pc[part, my_y, my_c, 0], pc[part, my_y, my_c, 1]]
        along = jnp.sum(cots[0] * values[:half_depth, :], axis=0, keepdims=True) + jnp.sum(
            cots[1] * values[half_depth:, :], axis=0, keepdims=True
        )
        factor = PROTOS / math.sqrt(total_crops)
        pull = along * (inv * inv * inv) * factor
        scale = inv * factor
        out_p[0, :, block] = cots[0] * scale - values[:half_depth, :] * pull
        out_p[1, :, block] = cots[1] * scale - values[half_depth:, :] * pull

    def along_y(way, step, half, t, part):
        view = out_p.at[half, :, columns(t, my_c, part)]
        peer = on_y(y_at(1 if way == 0 else -1))
        return remote(view, view, ring_sems.at[5, 0], yg_recv.at[part, way, step, half], peer)

    def hand_on(t, part):
        view = out_p.at[:, :, columns(t, my_c, part)]
        remote(view, view, ring_sems.at[6, 0], ring_sems.at[6, 1], sibling).start()

    def give_y(part):
        y_rings[part].finish()
        pull_columns(part)
        if ny == 4:
            for half in range(2):
                along_y(0, 0, half, my_y, part).start()
                along_y(1, 0, 1 - half, my_y, part).start()
        else:
            along_y(0, 1, 0, my_y, part).start()
            along_y(1, 1, 1, my_y, part).start()
        hand_on(my_y, part)

    give_y(0)

    def pull_rows(cot, first, count):
        values = emb[aligned(my_x * nz + my_z, share), :].astype(F32)
        values = values[first : first + count, :]
        inv = inv_norm(jnp.sum(values * values, axis=1, keepdims=True))
        along = jnp.sum(cot * values, axis=1, keepdims=True)
        factor = math.sqrt(PROTOS)
        out_e[my_x, my_z, pl.ds(first, count)] = cot * (inv * factor) - values * (
            along * (inv * inv * inv) * factor
        )

    late = pl.ds(first_share, rest)
    soon = pl.ds(0, first_share)

    def z_at(hops):
        return lax.rem(my_z + hops + nz, nz)

    def over_x_from(rel):
        view = out_e.at[my_x, z_at(rel), soon]
        for hop in far_first(nx):
            remote(
                view, view, ring_sems.at[9, 0], ring_sems.at[9, 1], on_x(x1[0].at(hop))
            ).start()

    def over_z_at(rel):
        view = out_e.at[my_x, my_z, soon]
        return remote(view, view, ring_sems.at[8, 0], zg_recv.at[rel], on_z(z_at(rel)))

    pull_rows(x2.finish(), first_share, rest)
    for hop in far_first(nx):
        view = out_e.at[my_x, my_z, late]
        remote(
            view, view, ring_sems.at[7, 0], ring_sems.at[7, 1], on_x(x1[0].at(hop))
        ).start()
    pull_rows(jnp.concatenate([scatter.finish() for scatter in z1], axis=0), 0, first_share)
    for hop in far_first(nz):
        over_z_at(hop).start()
    over_x_from(0)
    give_y(1)

    loss_z.start(loss_x.finish())

    def receive_z(rel):
        view = out_e.at[my_x, z_at(rel), soon]
        remote(view, view, ring_sems.at[8, 0], zg_recv.at[nz - rel], on_z(my_z)).wait_recv()
        over_x_from(rel)

    def send_late():
        arrived(out_e.at[pl.ds(0, nx - 1), 0, late], ring_sems.at[7], on_x(my_x))
        for hop in far_first(nz):
            view = out_e.at[:, my_z, late]
            remote(
                view, view, ring_sems.at[11, 0], ring_sems.at[11, 1], on_z(z_at(hop))
            ).start()

    def receive_y(way, step, half, part):
        t = y_at((-1 if way == 0 else 1) if step == 0 else ny // 2)
        view = out_p.at[half, :, columns(t, my_c, part)]
        remote(
            view, view, ring_sems.at[5, 0], yg_recv.at[part, way, step, half], on_y(my_y)
        ).wait_recv()

    def near_y(part, first):
        if ny == 4:
            for way in range(2):
                half = way if first else 1 - way
                t = y_at(-1 if way == 0 else 1)
                receive_y(way, 0, half, part)
                if first:
                    along_y(way, 1, half, t, part).start()
                else:
                    hand_on(t, part)

    pending = [nz - hop for hop in far_first(nz)]
    near_y(0, True)
    send_late()
    for rel in pending[: len(pending) // 2]:
        receive_z(rel)
    near_y(1, True)
    for rel in pending[len(pending) // 2 :]:
        receive_z(rel)
    near_y(0, False)
    near_y(1, False)
    for part in range(parts):
        for way in range(2):
            receive_y(way, 1, way, part)
        hand_on(y_at(ny // 2), part)
    out_l[0, 0] = jnp.sum(loss_z.finish()) / total_crops

    arrived(out_e.at[:, pl.ds(0, nz - 1), late], ring_sems.at[11], on_z(my_z))
    arrived(out_e.at[pl.ds(0, nx - 1), :, soon], ring_sems.at[9], on_x(my_x))
    own = out_p.at[:, :, pl.ds(0, ny * width)]
    arrived(own, ring_sems.at[6], sibling)
    departed(own, ring_sems.at[6], sibling)
    for g in range(groups):
        departed(h1.at[g, pl.ds(0, nx - 1)], x1_sems.at[g], on_x(my_x))
    for ring in (*z1, z2, x2):
        ring.close()
    for part in range(parts):
        departed(pc.at[part, pl.ds(0, ny - 1), 0], y_sems.at[part], on_y(my_y))
    remote(pc.at[:, :, 0], pc.at[:, :, 0], sib_send.at[0], sib_recv.at[0], sibling).wait_send()
    departed(out_p.at[:, :, pl.ds(0, (ny - 1) * width)], ring_sems.at[5], on_y(my_y))
    departed(out_e.at[pl.ds(0, nx - 1), 0, late], ring_sems.at[7], on_x(my_x))
    departed(out_e.at[0, pl.ds(0, nz - 1), soon], ring_sems.at[8], on_z(my_z))
    departed(out_e.at[pl.ds(0, nx - 1), :, soon], ring_sems.at[9], on_x(my_x))
    departed(out_e.at[:, pl.ds(0, nz - 1), late], ring_sems.at[11], on_z(my_z))


def local(sizes, embeddings, queue, prototypes, pairing):
    ny, nx, nz = sizes
    dp_count = ny * CORES
    crops, depth = embeddings.shape
    rows = crops + queue.shape[0]
    cols = prototypes.shape[1]
    width = cols // dp_count
    share = crops // (nx * nz)
    rest = share // 4
    row_blocks, crop_blocks, lane_blocks = rows // 128, crops // 128, cols // 128
    half = depth // 2
    tile = 256
    dma = pltpu.SemaphoreType.DMA
    vmem = pltpu.VMEM
    scratch = [
        vmem((crops, depth), BF16),
        vmem((rows - crops, depth), BF16),
        vmem((depth, cols), BF16),
        vmem((1, crops), jnp.int32),
        vmem((rows, cols), F32),
        vmem((crops, cols), F32),
        vmem((crops, cols), F32),
        vmem((rows, depth), BF16),
        vmem((crops, depth), BF16),
        vmem((depth, cols), BF16),
        vmem((depth, crops), BF16),
        vmem((cols, depth), BF16),
        vmem((crops, cols), BF16),
        vmem((cols // tile, 8, tile), F32),
        vmem((row_blocks, 128), F32),
        vmem((crops, 128), F32),
        vmem((rows, 128), F32),
        vmem((crops, 128), F32),
        vmem((crops, 128), F32),
        vmem((ITERS, dp_count, lane_blocks, 128), F32),
        vmem((ITERS, nx, row_blocks, 128), F32),
        vmem((ITERS, nz, row_blocks, 128), F32),
        vmem((nx, crop_blocks, 128), F32),
        vmem((nz, crop_blocks, 128), F32),
        vmem((dp_count, 8, 128), F32),
        vmem((nx, 8, 128), F32),
        vmem((nz, 8, 128), F32),
        vmem((2, ny, CORES, 2, half, width // 2), F32),
        vmem((ny, 2, 2, half, width // 2), F32),
        vmem((2, 2, 2, 2, half, width // 2), F32),
        vmem((3, nx, nz, rest, depth), F32),
        vmem((nz, nx, rest, depth), F32),
        vmem((3, 2, 2, 2, nz // 2, rest, depth), F32),
        vmem((3, nz - 1, rest, depth), F32),
        vmem((nz - 1, nx, rest, depth), F32),
        vmem((nx - 1, rest, depth), F32),
        dma((4,)),
        dma((ITERS, 2)),
        dma((ITERS, 2)),
        dma((ITERS, 2)),
        dma((2, 2)),
        dma((3, 2)),
        dma((1,)),
        dma((ny,)),
        dma((2, 2)),
        dma((2, 2, 2)),
        dma((12, 2)),
        dma((3, 2)),
        dma((3, 2, 2)),
        dma((3, 2)),
        dma((2, 2, 2, 2)),
        dma((nz,)),
    ]
    in_vmem = pl.BlockSpec(memory_space=pltpu.VMEM)
    anywhere = pl.BlockSpec(memory_space=pl.ANY)
    grad_embed, grad_proto, loss = pl.pallas_call(
        functools.partial(kernel, sizes),
        out_shape=(
            pltpu.VMEM((nx, nz, share, depth), F32),
            pltpu.VMEM((2, half, cols), F32),
            jax.ShapeDtypeStruct((1, 1), F32),
        ),
        in_specs=[anywhere] * 4,
        out_specs=(in_vmem, in_vmem, pl.BlockSpec(memory_space=pltpu.SMEM)),
        scratch_shapes=scratch,
        compiler_params=pltpu.CompilerParams(
            collective_id=0, has_side_effects=True, vmem_limit_bytes=59 * 1024 * 1024
        ),
    )(embeddings, queue, prototypes, pairing.reshape(1, crops))
    return (
        grad_embed.reshape(crops, depth),
        grad_proto.reshape(depth, cols),
        loss.reshape(()),
    )


def solution(mesh):
    nx = ALONG_X
    sizes = (mesh.shape["dp"] // CORES, nx, mesh.shape["proto"] // nx)
    return jax.shard_map(
        functools.partial(local, sizes),
        mesh=mesh,
        in_specs=(P("dp", None), P("dp", None), P(None, "proto"), P("dp")),
        out_specs=(P("dp", None), P(None, "proto"), P()),
        check_vma=False,
    )
```

```python
import functools
import math

import jax
import jax.numpy as jnp
from jax import lax
from jax.experimental import pallas as pl
from jax.experimental.pallas import tpu as pltpu
from jax.sharding import PartitionSpec as P

PROTOS = 65536
ITERS = 3
CORES = 2
ALONG_X = 4
LOG2E = math.log2(math.e)
F32 = jnp.float32
BF16 = jnp.bfloat16
MESH = pl.DeviceIdType.MESH


def inv_norm(sum_sq):
    shifted = sum_sq + 1e-06
    guess = lax.rsqrt(shifted)
    return guess * (1.5 - 0.5 * shifted * guess * guess)


def aligned(index, size):
    return pl.ds(pl.multiple_of(index * size, size), size)


def remote(src, dst, send_sem, recv_sem, device):
    return pltpu.make_async_remote_copy(
        src_ref=src,
        dst_ref=dst,
        send_sem=send_sem,
        recv_sem=recv_sem,
        device_id=device,
        device_id_type=MESH,
    )


def arrived(view, sems, device):
    remote(view, view, sems.at[0], sems.at[1], device).wait_recv()


def departed(view, sems, device):
    remote(view, view, sems.at[0], sems.at[1], device).wait_send()


def far_first(size):
    return sorted(range(1, size), key=lambda hop: (-min(hop, size - hop), hop))


class Exchange:
    def __init__(self, buf, sems, me, size, device):
        self.buf, self.sems, self.me, self.size, self.device = buf, sems, me, size, device

    def start(self, block):
        self.buf[self.me] = block
        for hop in far_first(self.size):
            slot = self.buf.at[self.me]
            peer = self.device(lax.rem(self.me + hop, self.size))
            remote(slot, slot, self.sems.at[0], self.sems.at[1], peer).start()

    def finish(self):
        others = self.buf.at[pl.ds(0, self.size - 1)]
        arrived(others, self.sems, self.device(self.me))
        departed(others, self.sems, self.device(self.me))
        total = self.buf[0]
        for slot in range(1, self.size):
            total = total + self.buf[slot]
        return total


class Scatter:
    def __init__(self, n, me, part, recv, sems, device):
        self.n, self.me, self.part, self.recv = n, me, part, recv
        self.sems, self.device = sems, device

    def start(self):
        for hop in far_first(self.n):
            piece = lax.rem(self.me + hop, self.n)
            remote(
                self.part(piece),
                self.recv.at[hop - 1],
                self.sems.at[0],
                self.sems.at[1],
                self.device(piece),
            ).start()

    def finish(self):
        arrived(self.recv, self.sems, self.device(self.me))
        total = self.part(self.me)[...]
        for hop in range(1, self.n):
            total = total + self.recv[hop - 1]
        return total

    def close(self):
        departed(self.recv, self.sems, self.device(self.me))


class Ring:
    def __init__(self, n, me, part, recv, sems, recv_sems, device):
        self.n, self.me, self.part, self.recv = n, me, part, recv
        self.sems, self.recv_sems, self.device = sems, recv_sems, device
        self.far = n // 2

    def at(self, hops):
        return lax.rem(self.me + hops + self.n, self.n)

    def copy(self, way, step, half, piece):
        return remote(
            self.part(piece, half),
            self.recv.at[way, step, half],
            self.sems.at[0],
            self.recv_sems.at[way, step],
            self.device(self.at(1 if way == 0 else -1)),
        )

    def add(self, way, step, half, piece):
        view = self.part(piece, half)
        view[...] = view[...] + self.recv[way, step, half]

    def first(self):
        for way in range(2):
            self.copy(way, 0, way, self.at(self.far)).start()

    def early(self, way):
        if self.far == 2:
            self.copy(way, 1, 1 - way, self.at(1 if way == 0 else -1)).start()

    def second(self):
        if self.far == 2:
            for way in range(2):
                piece = self.at(1 if way == 0 else -1)
                self.copy(way, 0, way, piece).wait_recv()
                self.add(way, 0, way, piece)
                self.copy(way, 1, way, piece).start()

    def finish(self):
        for way in range(2):
            if self.far == 2:
                view = self.recv.at[way, 1]
                remote(
                    view,
                    view,
                    self.sems.at[0],
                    self.recv_sems.at[way, 1],
                    self.device(self.me),
                ).wait_recv()
                self.add(way, 1, 0, self.me)
                self.add(way, 1, 1, self.me)
            else:
                self.copy(way, 0, way, self.me).wait_recv()
                self.add(way, 0, way, self.me)


def kernel(
    sizes,
    emb_hbm,
    que_hbm,
    pro_hbm,
    pair_hbm,
    out_e,
    out_p,
    out_l,
    emb,
    que,
    pro,
    pair,
    ex,
    sx,
    yx,
    rows_bf,
    part_bf,
    pro_bf,
    emb_t,
    pro_t,
    differ,
    colacc,
    dense,
    softp,
    rbc,
    stb,
    qpart,
    dpbuf,
    xbuf,
    zbuf,
    sxbuf,
    szbuf,
    ldp,
    lx,
    lz,
    pc,
    sib,
    yrecv,
    h1,
    h2,
    x1recv,
    z1recv,
    z2recv,
    x2recv,
    load_sems,
    dp_sems,
    x_sems,
    z_sems,
    soft_sems,
    loss_sems,
    sib_send,
    sib_recv,
    y_sems,
    y_pairs,
    ring_sems,
    x1_sems,
    x1_pairs,
    z1_sems,
    yg_recv,
    zg_recv,
):
    ny, nx, nz = sizes
    dp_count = ny * CORES
    crops, depth = emb.shape
    rows = crops + que.shape[0]
    cols = pro.shape[1]
    total_rows = rows * dp_count
    total_crops = crops * dp_count
    lane_blocks = cols // 128
    row_blocks = rows // 128
    crop_blocks = crops // 128
    width = cols // dp_count
    tile = 256

    my_dp = lax.axis_index("dp")
    my_proto = lax.axis_index("proto")
    my_y, my_c = my_dp // CORES, lax.rem(my_dp, CORES)
    my_z, my_x = my_proto // nx, lax.rem(my_proto, nx)

    def on_dp(index):
        return (index, my_proto)

    def on_x(index):
        return (my_dp, my_z * nx + index)

    def on_z(index):
        return (my_dp, index * nx + my_x)

    def on_y(index):
        return (index * CORES + my_c, my_proto)

    sibling = (my_y * CORES + 1 - my_c, my_proto)

    loads = [
        pltpu.make_async_copy(source, target, load_sems.at[i])
        for i, (source, target) in enumerate(
            ((emb_hbm, emb), (que_hbm, que), (pro_hbm, pro), (pair_hbm, pair))
        )
    ]
    for load in loads:
        load.start()
    barrier = pltpu.get_barrier_semaphore()
    for me, size, device in ((my_z, nz, on_z), (my_x, nx, on_x), (my_dp, dp_count, on_dp)):
        for hop in far_first(size):
            pl.semaphore_signal(
                barrier, inc=1, device_id=device(lax.rem(me + hop, size)), device_id_type=MESH
            )

    loads[0].wait()
    loads[1].wait()

    @pl.loop(0, crops // tile)
    def _(i):
        block = aligned(i, tile)
        for source, first in ((emb, 0), (que, crops)):
            values = source[block, :].astype(F32)
            inv = inv_norm(jnp.sum(values * values, axis=1, keepdims=True))
            start = pl.multiple_of(first + i * tile, tile)
            rows_bf[pl.ds(start, tile), :] = (values * inv).astype(BF16)

    loads[2].wait()
    loads[3].wait()

    @pl.loop(0, cols // tile)
    def _(j):
        block = aligned(j, tile)
        values = pro[:, block].astype(F32)
        inv = inv_norm(jnp.sum(values * values, axis=0, keepdims=True))
        pro_bf[:, block] = (values * inv).astype(BF16)

    softp[...] = jnp.zeros_like(softp)

    @pl.loop(0, cols // tile)
    def _(j):
        block = aligned(j, tile)
        weights = pro_bf[:, block]
        acc = jnp.zeros((8, tile), F32)
        for i in range(rows // tile):
            lines = slice(i * tile, (i + 1) * tile)
            scores = jnp.dot(rows_bf[lines, :], weights, preferred_element_type=F32)
            if i < crops // tile:
                sx[lines, block] = scores
                soft = jnp.exp2(scores * (10.0 * LOG2E))
                folded = soft[:, :128]
                for k in range(1, tile // 128):
                    folded = folded + soft[:, k * 128 : (k + 1) * 128]
                softp[lines, :] += folded
                expo = soft * soft
            else:
                expo = jnp.exp2(scores * (20.0 * LOG2E))
            ex[lines, block] = expo
            acc = acc + jnp.sum(expo.reshape(tile // 8, 8, tile), axis=0)
        colacc[j] = acc

    def dense_cols():
        pieces = []
        for j in range(lane_blocks):
            k, part = j * 128 // tile, (j * 128) % tile
            pieces.append(jnp.sum(colacc[k, :, part : part + 128], axis=0, keepdims=True))
        return jnp.concatenate(pieces, axis=0)

    def dense_rows(source, blocks):
        pieces = []
        for b in range(blocks):
            pieces.append(
                jnp.sum(source[b * 128 : (b + 1) * 128, :].T, axis=0, keepdims=True)
            )
        return jnp.concatenate(pieces, axis=0)

    def spread_rows(target, dense, blocks, first=0):
        for b in range(blocks):
            target[(first + b) * 128 : (first + b + 1) * 128, :] = jnp.broadcast_to(
                dense[b : b + 1, :], (128, 128)
            ).T

    def col_pass(first, last, accs):
        groups = 4

        def step(i, accs):
            accs = list(accs)
            for g in range(groups):
                lines = pl.ds(pl.multiple_of(i * 8 * groups + 8 * g, 8), 8)
                scale = rbc[lines, :]
                for j in range(lane_blocks):
                    accs[j] = accs[j] + ex[lines, j * 128 : (j + 1) * 128] * scale
            return tuple(accs)

        return lax.fori_loop(first // (8 * groups), last // (8 * groups), step, accs)

    def spread_cols(dense):
        return [
            jnp.broadcast_to(dense[j : j + 1, :], (8, 128)) for j in range(lane_blocks)
        ]

    def row_sums(target, start, count, line_sums):
        pair = 2

        @pl.loop(start // (128 * pair), (start + count) // (128 * pair))
        def _(i):
            for k in range(pair):
                first = (i * pair + k) * 128
                accs = [
                    line_sums(pl.ds(pl.multiple_of(first + 8 * g, 8), 8)) for g in range(16)
                ]
                turned = jnp.concatenate(accs, axis=0).T
                target[pl.ds(i * pair + k, 1), :] = jnp.sum(turned, axis=0, keepdims=True)

    def row_pass(scales, start, count):
        def line_sums(lines):
            acc = ex[lines, :128] * scales[0]
            for j in range(1, lane_blocks):
                acc = acc + ex[lines, j * 128 : (j + 1) * 128] * scales[j]
            return acc

        row_sums(dense, start, count, line_sums)

    def partner_pass(scales):
        def line_sums(lines):
            acc = jnp.zeros((8, 128), F32)
            for j in range(lane_blocks):
                block = slice(j * 128, (j + 1) * 128)
                code = yx[lines, block] * scales[j]
                yx[lines, block] = code
                acc = acc + code
            return acc

        row_sums(dense, 0, crops, line_sums)

    def soften(first, last):
        groups = 2

        @pl.loop(first // (8 * groups), last // (8 * groups))
        def _(i):
            for g in range(groups):
                lines = pl.ds(pl.multiple_of(i * 8 * groups + 8 * g, 8), 8)
                scale = stb[lines, :]
                acc = jnp.zeros((8, 128), F32)
                for j in range(lane_blocks):
                    block = slice(j * 128, (j + 1) * 128)
                    score = sx[lines, block]
                    acc = acc + yx[lines, block] * score
                    sx[lines, block] = jnp.exp2(score * (10.0 * LOG2E)) * scale
                qpart[lines, :] = acc

    def pick_partners():
        local_pair = pair[...] - my_dp * crops

        @pl.loop(0, crops // tile)
        def _(i):
            block = aligned(i, tile)
            line = lax.broadcasted_iota(jnp.int32, (tile, crops), 0) + i * tile
            pick = jnp.where(line == local_pair, 1.0, 0.0).astype(BF16)
            part_bf[block, :] = jnp.dot(
                pick, rows_bf[:crops, :], preferred_element_type=F32
            ).astype(BF16)

    def partner_exponents():
        @pl.loop(0, cols // tile)
        def _(j):
            block = aligned(j, tile)
            weights = pro_bf[:, block]
            for i in range(crops // tile):
                lines = slice(i * tile, (i + 1) * tile)
                scores = jnp.dot(part_bf[lines, :], weights, preferred_element_type=F32)
                soft = jnp.exp2(scores * (10.0 * LOG2E))
                yx[lines, block] = soft * soft

    def transposed_rows():
        @pl.loop(0, crops // tile)
        def _(i):
            block = aligned(i, tile)
            emb_t[:, block] = rows_bf[block, :].astype(F32).T.astype(BF16)

    def transposed_cols():
        @pl.loop(0, cols // tile)
        def _(j):
            block = aligned(j, tile)
            pro_t[block, :] = pro_bf[:, block].astype(F32).T.astype(BF16)

    pl.semaphore_wait(barrier, dp_count - 1 + nx - 1 + nz - 1)
    col_dense = dense_cols()
    soft_total = None
    row_sum = None
    soft_x = Exchange(sxbuf, soft_sems.at[0], my_x, nx, on_x)
    soft_z = Exchange(szbuf, soft_sems.at[1], my_z, nz, on_z)
    half_blocks = row_blocks // 2
    for it in range(ITERS):
        over_dp = Exchange(dpbuf.at[it], dp_sems.at[it], my_dp, dp_count, on_dp)
        over_x = [
            Exchange(
                xbuf.at[it, :, pl.ds(h * half_blocks, half_blocks)],
                x_sems.at[it, h],
                my_x,
                nx,
                on_x,
            )
            for h in range(2)
        ]
        over_z = [
            Exchange(
                zbuf.at[it, :, pl.ds(h * half_blocks, half_blocks)],
                z_sems.at[it, h],
                my_z,
                nz,
                on_z,
            )
            for h in range(2)
        ]
        over_dp.start(col_dense)
        if it == 0:
            pick_partners()
            soft_part = dense_rows(softp, crop_blocks)
        elif it == 1:
            soft_x.start(soft_part)
            transposed_cols()
        else:
            soft_total = soft_z.finish()
            spread_rows(stb, 10.0 / soft_total, crop_blocks)
        col_scale = 1.0 / (PROTOS * over_dp.finish())
        if it < ITERS - 1:
            scales = spread_cols(col_scale)
            for h in range(2):
                row_pass(scales, h * (rows // 2), rows // 2)
                over_x[h].start(dense[h * half_blocks : (h + 1) * half_blocks, :])
            if it == 0:
                transposed_rows()
            else:
                soft_z.start(soft_x.finish())
            for h in range(2):
                over_z[h].start(over_x[h].finish())
            if it == 0:
                partner_exponents()
            accs = (jnp.zeros((8, 128), F32),) * lane_blocks
            for h in range(2):
                scale = 1.0 / (total_rows * over_z[h].finish())
                spread_rows(rbc, scale, half_blocks, h * half_blocks)
                accs = col_pass(h * (rows // 2), (h + 1) * (rows // 2), accs)
            col_dense = jnp.concatenate(
                [jnp.sum(a, axis=0, keepdims=True) for a in accs], axis=0
            )
        else:
            partner_pass(spread_cols(10.0 * col_scale))
            over_x[0].start(dense[:crop_blocks, :])
            soften(0, crops // 2)
            over_z[0].start(over_x[0].finish())
            soften(crops // 2, crops)
            row_sum = over_z[0].finish()

    spread_rows(rbc, 10.0 / row_sum, crop_blocks)

    share = crops // (nx * nz)
    rest = share // 4
    groups = 3
    first_share = groups * rest
    x_line = nz * share

    def x_ring(g):
        return Ring(
            nx,
            my_x,
            lambda t, half: h1.at[g, t, pl.ds(half * (nz // 2), nz // 2)],
            x1recv.at[g],
            x1_sems.at[g],
            x1_pairs.at[g],
            on_x,
        )

    def z_scatter(g):
        return Scatter(nz, my_z, lambda t: h1.at[g, my_x, t], z1recv.at[g], z1_sems.at[g], on_z)

    x1 = [x_ring(g) for g in range(groups)]
    z1 = [z_scatter(g) for g in range(groups)]
    z2 = Scatter(nz, my_z, lambda t: h2.at[t], z2recv, ring_sems.at[2], on_z)
    x2 = Scatter(nx, my_x, lambda t: h2.at[my_z, t], x2recv, ring_sems.at[3], on_x)

    repeat = tile // 128
    for hops in [nx // 2] + ([1, -1] if nx == 4 else []) + [0]:
        t = x1[0].at(hops)
        lines = aligned(t, x_line)
        scale = jnp.concatenate([rbc[lines, :]] * repeat, axis=1)
        for j in range(cols // tile):
            block = slice(j * tile, (j + 1) * tile)
            value = sx[lines, block] - yx[lines, block] * scale
            differ[lines, block] = value.astype(BF16)
        cot = jnp.dot(differ[lines, :], pro_t[...], preferred_element_type=F32)
        for pz in range(nz):
            for g in range(groups):
                first = pz * share + g * rest
                h1[g, t, pz] = cot[first : first + rest, :]
            h2[pz, t] = cot[pz * share + first_share : (pz + 1) * share, :]
        for ring in x1:
            if hops == nx // 2:
                ring.first()
            elif hops == 1:
                ring.early(0)
            elif hops == -1:
                ring.early(1)
    z2.start()

    half_depth = depth // 2
    parts = 2
    narrow = width // parts

    def piece(t, core):
        block = aligned(t * CORES + core, width)
        cot = jnp.dot(emb_t[...], differ[:, block], preferred_element_type=F32)
        for part in range(parts):
            across = slice(part * narrow, (part + 1) * narrow)
            pc[part, t, core, 0] = cot[:half_depth, across]
            pc[part, t, core, 1] = cot[half_depth:, across]

    def to_sibling(number, t):
        return remote(
            pc.at[:, t, 1 - my_c], sib.at[number], sib_send.at[0], sib_recv.at[number], sibling
        )

    def y_ring_of(part):
        return Ring(
            ny,
            my_y,
            lambda t, half: pc.at[part, t, my_c, half],
            yrecv.at[part],
            y_sems.at[part],
            y_pairs.at[part],
            on_y,
        )

    y_rings = [y_ring_of(part) for part in range(parts)]
    y_at = y_rings[0].at
    near = [1, -1] if ny == 4 else []
    order = [ny // 2] + near + [0]
    for number, hops in enumerate(order):
        t = y_at(hops)
        piece(t, 1 - my_c)
        to_sibling(number, t).start()
        piece(t, my_c)
        to_sibling(number, t).wait_recv()
        for part in range(parts):
            pc[part, t, my_c] = pc[part, t, my_c] + sib[number, part]
        if hops == ny // 2:
            y_rings[0].first()
        elif hops == 1:
            y_rings[0].early(0)
        elif hops == -1:
            y_rings[0].early(1)
    y_rings[1].first()

    def add_up(i, acc):
        lines = aligned(i, 8)
        return acc + qpart[lines, :] * rbc[lines, :]

    code_score = lax.fori_loop(0, crops // 8, add_up, jnp.zeros((8, 128), F32))
    log_total = jnp.log(soft_total) * (1.0 / (nx * nz))
    if crop_blocks != 8:
        log_total = jnp.broadcast_to(jnp.sum(log_total, axis=0, keepdims=True), (8, 128)) / 8.0
    loss_dp = Exchange(ldp, loss_sems.at[0], my_dp, dp_count, on_dp)
    loss_x = Exchange(lx, loss_sems.at[1], my_x, nx, on_x)
    loss_z = Exchange(lz, loss_sems.at[2], my_z, nz, on_z)
    loss_dp.start(log_total - code_score)

    for ring in x1:
        ring.second()
    y_rings[0].second()
    y_rings[1].early(0)
    y_rings[1].early(1)
    for ring, scatter in zip(x1, z1):
        ring.finish()
        scatter.start()
        if ring is x1[0]:
            y_rings[1].second()
    h2[my_z] = z2.finish()
    x2.start()
    loss_x.start(loss_dp.finish())

    def columns(t, core, part):
        first = (t * CORES + core) * width + part * narrow
        return pl.ds(pl.multiple_of(first, narrow), narrow)

    def pull_columns(part):
        block = columns(my_y, my_c, part)
        values = pro[:, block].astype(F32)
        inv = inv_norm(jnp.sum(values * values, axis=0, keepdims=True))
        cots = [pc[part, my_y, my_c, 0], pc[part, my_y, my_c, 1]]
        along = jnp.sum(cots[0] * values[:half_depth, :], axis=0, keepdims=True) + jnp.sum(
            cots[1] * values[half_depth:, :], axis=0, keepdims=True
        )
        factor = PROTOS / math.sqrt(total_crops)
        pull = along * (inv * inv * inv) * factor
        scale = inv * factor
        out_p[0, :, block] = cots[0] * scale - values[:half_depth, :] * pull
        out_p[1, :, block] = cots[1] * scale - values[half_depth:, :] * pull

    def along_y(way, step, half, t, part):
        view = out_p.at[half, :, columns(t, my_c, part)]
        peer = on_y(y_at(1 if way == 0 else -1))
        return remote(view, view, ring_sems.at[5, 0], yg_recv.at[part, way, step, half], peer)

    def hand_on(t, part):
        view = out_p.at[:, :, columns(t, my_c, part)]
        remote(view, view, ring_sems.at[6, 0], ring_sems.at[6, 1], sibling).start()

    def give_y(part):
        y_rings[part].finish()
        pull_columns(part)
        if ny == 4:
            for half in range(2):
                along_y(0, 0, half, my_y, part).start()
                along_y(1, 0, 1 - half, my_y, part).start()
        else:
            along_y(0, 1, 0, my_y, part).start()
            along_y(1, 1, 1, my_y, part).start()
        hand_on(my_y, part)

    give_y(0)

    def pull_rows(cot, first, count):
        values = emb[aligned(my_x * nz + my_z, share), :].astype(F32)
        values = values[first : first + count, :]
        inv = inv_norm(jnp.sum(values * values, axis=1, keepdims=True))
        along = jnp.sum(cot * values, axis=1, keepdims=True)
        factor = math.sqrt(PROTOS)
        out_e[my_x, my_z, pl.ds(first, count)] = cot * (inv * factor) - values * (
            along * (inv * inv * inv) * factor
        )

    late = pl.ds(first_share, rest)
    soon = pl.ds(0, first_share)

    def z_at(hops):
        return lax.rem(my_z + hops + nz, nz)

    def over_x_from(rel):
        view = out_e.at[my_x, z_at(rel), soon]
        for hop in far_first(nx):
            remote(
                view, view, ring_sems.at[9, 0], ring_sems.at[9, 1], on_x(x1[0].at(hop))
            ).start()

    def over_z_at(rel):
        view = out_e.at[my_x, my_z, soon]
        return remote(view, view, ring_sems.at[8, 0], zg_recv.at[rel], on_z(z_at(rel)))

    pull_rows(x2.finish(), first_share, rest)
    for hop in far_first(nx):
        view = out_e.at[my_x, my_z, late]
        remote(
            view, view, ring_sems.at[7, 0], ring_sems.at[7, 1], on_x(x1[0].at(hop))
        ).start()
    give_y(1)
    pull_rows(jnp.concatenate([scatter.finish() for scatter in z1], axis=0), 0, first_share)
    for hop in far_first(nz):
        over_z_at(hop).start()
    over_x_from(0)

    loss_z.start(loss_x.finish())

    def receive_z(rel):
        view = out_e.at[my_x, z_at(rel), soon]
        remote(view, view, ring_sems.at[8, 0], zg_recv.at[nz - rel], on_z(my_z)).wait_recv()
        over_x_from(rel)

    def send_late():
        arrived(out_e.at[pl.ds(0, nx - 1), 0, late], ring_sems.at[7], on_x(my_x))
        for hop in far_first(nz):
            view = out_e.at[:, my_z, late]
            remote(
                view, view, ring_sems.at[11, 0], ring_sems.at[11, 1], on_z(z_at(hop))
            ).start()

    def receive_y(way, step, half, part):
        t = y_at((-1 if way == 0 else 1) if step == 0 else ny // 2)
        view = out_p.at[half, :, columns(t, my_c, part)]
        remote(
            view, view, ring_sems.at[5, 0], yg_recv.at[part, way, step, half], on_y(my_y)
        ).wait_recv()

    def near_y(part, first):
        if ny == 4:
            for way in range(2):
                half = way if first else 1 - way
                t = y_at(-1 if way == 0 else 1)
                receive_y(way, 0, half, part)
                if first:
                    along_y(way, 1, half, t, part).start()
                else:
                    hand_on(t, part)

    pending = [nz - hop for hop in far_first(nz)]
    near_y(0, True)
    near_y(1, True)
    send_late()
    for rel in pending:
        receive_z(rel)
    near_y(0, False)
    near_y(1, False)
    for part in range(parts):
        for way in range(2):
            receive_y(way, 1, way, part)
        hand_on(y_at(ny // 2), part)
    out_l[0, 0] = jnp.sum(loss_z.finish()) / total_crops

    arrived(out_e.at[:, pl.ds(0, nz - 1), late], ring_sems.at[11], on_z(my_z))
    arrived(out_e.at[pl.ds(0, nx - 1), :, soon], ring_sems.at[9], on_x(my_x))
    own = out_p.at[:, :, pl.ds(0, ny * width)]
    arrived(own, ring_sems.at[6], sibling)
    departed(own, ring_sems.at[6], sibling)
    for g in range(groups):
        departed(h1.at[g, pl.ds(0, nx - 1)], x1_sems.at[g], on_x(my_x))
    for ring in (*z1, z2, x2):
        ring.close()
    for part in range(parts):
        departed(pc.at[part, pl.ds(0, ny - 1), 0], y_sems.at[part], on_y(my_y))
    remote(pc.at[:, :, 0], pc.at[:, :, 0], sib_send.at[0], sib_recv.at[0], sibling).wait_send()
    departed(out_p.at[:, :, pl.ds(0, (ny - 1) * width)], ring_sems.at[5], on_y(my_y))
    departed(out_e.at[pl.ds(0, nx - 1), 0, late], ring_sems.at[7], on_x(my_x))
    departed(out_e.at[0, pl.ds(0, nz - 1), soon], ring_sems.at[8], on_z(my_z))
    departed(out_e.at[pl.ds(0, nx - 1), :, soon], ring_sems.at[9], on_x(my_x))
    departed(out_e.at[:, pl.ds(0, nz - 1), late], ring_sems.at[11], on_z(my_z))


def local(sizes, embeddings, queue, prototypes, pairing):
    ny, nx, nz = sizes
    dp_count = ny * CORES
    crops, depth = embeddings.shape
    rows = crops + queue.shape[0]
    cols = prototypes.shape[1]
    width = cols // dp_count
    share = crops // (nx * nz)
    rest = share // 4
    row_blocks, crop_blocks, lane_blocks = rows // 128, crops // 128, cols // 128
    half = depth // 2
    tile = 256
    dma = pltpu.SemaphoreType.DMA
    vmem = pltpu.VMEM
    scratch = [
        vmem((crops, depth), BF16),
        vmem((rows - crops, depth), BF16),
        vmem((depth, cols), BF16),
        vmem((1, crops), jnp.int32),
        vmem((rows, cols), F32),
        vmem((crops, cols), F32),
        vmem((crops, cols), F32),
        vmem((rows, depth), BF16),
        vmem((crops, depth), BF16),
        vmem((depth, cols), BF16),
        vmem((depth, crops), BF16),
        vmem((cols, depth), BF16),
        vmem((crops, cols), BF16),
        vmem((cols // tile, 8, tile), F32),
        vmem((row_blocks, 128), F32),
        vmem((crops, 128), F32),
        vmem((rows, 128), F32),
        vmem((crops, 128), F32),
        vmem((crops, 128), F32),
        vmem((ITERS, dp_count, lane_blocks, 128), F32),
        vmem((ITERS, nx, row_blocks, 128), F32),
        vmem((ITERS, nz, row_blocks, 128), F32),
        vmem((nx, crop_blocks, 128), F32),
        vmem((nz, crop_blocks, 128), F32),
        vmem((dp_count, 8, 128), F32),
        vmem((nx, 8, 128), F32),
        vmem((nz, 8, 128), F32),
        vmem((2, ny, CORES, 2, half, width // 2), F32),
        vmem((ny, 2, 2, half, width // 2), F32),
        vmem((2, 2, 2, 2, half, width // 2), F32),
        vmem((3, nx, nz, rest, depth), F32),
        vmem((nz, nx, rest, depth), F32),
        vmem((3, 2, 2, 2, nz // 2, rest, depth), F32),
        vmem((3, nz - 1, rest, depth), F32),
        vmem((nz - 1, nx, rest, depth), F32),
        vmem((nx - 1, rest, depth), F32),
        dma((4,)),
        dma((ITERS, 2)),
        dma((ITERS, 2, 2)),
        dma((ITERS, 2, 2)),
        dma((2, 2)),
        dma((3, 2)),
        dma((1,)),
        dma((ny,)),
        dma((2, 2)),
        dma((2, 2, 2)),
        dma((12, 2)),
        dma((3, 2)),
        dma((3, 2, 2)),
        dma((3, 2)),
        dma((2, 2, 2, 2)),
        dma((nz,)),
    ]
    in_vmem = pl.BlockSpec(memory_space=pltpu.VMEM)
    anywhere = pl.BlockSpec(memory_space=pl.ANY)
    grad_embed, grad_proto, loss = pl.pallas_call(
        functools.partial(kernel, sizes),
        out_shape=(
            pltpu.VMEM((nx, nz, share, depth), F32),
            pltpu.VMEM((2, half, cols), F32),
            jax.ShapeDtypeStruct((1, 1), F32),
        ),
        in_specs=[anywhere] * 4,
        out_specs=(in_vmem, in_vmem, pl.BlockSpec(memory_space=pltpu.SMEM)),
        scratch_shapes=scratch,
        compiler_params=pltpu.CompilerParams(
            collective_id=0, has_side_effects=True, vmem_limit_bytes=59 * 1024 * 1024
        ),
    )(embeddings, queue, prototypes, pairing.reshape(1, crops))
    return (
        grad_embed.reshape(crops, depth),
        grad_proto.reshape(depth, cols),
        loss.reshape(()),
    )


def solution(mesh):
    nx = ALONG_X
    sizes = (mesh.shape["dp"] // CORES, nx, mesh.shape["proto"] // nx)
    return jax.shard_map(
        functools.partial(local, sizes),
        mesh=mesh,
        in_specs=(P("dp", None), P("dp", None), P(None, "proto"), P("dp")),
        out_specs=(P("dp", None), P(None, "proto"), P()),
        check_vma=False,
    )
```

```python
import functools
import math

import jax
import jax.numpy as jnp
from jax import lax
from jax.experimental import pallas as pl
from jax.experimental.pallas import tpu as pltpu
from jax.sharding import PartitionSpec as P

PROTOS = 65536
ITERS = 3
CORES = 2
ALONG_X = 4
LOG2E = math.log2(math.e)
F32 = jnp.float32
BF16 = jnp.bfloat16
MESH = pl.DeviceIdType.MESH


def inv_norm(sum_sq):
    shifted = sum_sq + 1e-06
    guess = lax.rsqrt(shifted)
    return guess * (1.5 - 0.5 * shifted * guess * guess)


def aligned(index, size):
    return pl.ds(pl.multiple_of(index * size, size), size)


def remote(src, dst, send_sem, recv_sem, device):
    return pltpu.make_async_remote_copy(
        src_ref=src,
        dst_ref=dst,
        send_sem=send_sem,
        recv_sem=recv_sem,
        device_id=device,
        device_id_type=MESH,
    )


def arrived(view, sems, device):
    remote(view, view, sems.at[0], sems.at[1], device).wait_recv()


def departed(view, sems, device):
    remote(view, view, sems.at[0], sems.at[1], device).wait_send()


def far_first(size):
    return sorted(range(1, size), key=lambda hop: (-min(hop, size - hop), hop))


class Exchange:
    def __init__(self, buf, sems, me, size, device):
        self.buf, self.sems, self.me, self.size, self.device = buf, sems, me, size, device

    def start(self, block):
        self.buf[self.me] = block
        for hop in far_first(self.size):
            slot = self.buf.at[self.me]
            peer = self.device(lax.rem(self.me + hop, self.size))
            remote(slot, slot, self.sems.at[0], self.sems.at[1], peer).start()

    def finish(self):
        others = self.buf.at[pl.ds(0, self.size - 1)]
        arrived(others, self.sems, self.device(self.me))
        departed(others, self.sems, self.device(self.me))
        total = self.buf[0]
        for slot in range(1, self.size):
            total = total + self.buf[slot]
        return total


class Scatter:
    def __init__(self, n, me, part, recv, sems, device):
        self.n, self.me, self.part, self.recv = n, me, part, recv
        self.sems, self.device = sems, device

    def start(self):
        for hop in far_first(self.n):
            piece = lax.rem(self.me + hop, self.n)
            remote(
                self.part(piece),
                self.recv.at[hop - 1],
                self.sems.at[0],
                self.sems.at[1],
                self.device(piece),
            ).start()

    def finish(self):
        arrived(self.recv, self.sems, self.device(self.me))
        total = self.part(self.me)[...]
        for hop in range(1, self.n):
            total = total + self.recv[hop - 1]
        return total

    def close(self):
        departed(self.recv, self.sems, self.device(self.me))


class Ring:
    def __init__(self, n, me, part, recv, sems, recv_sems, device):
        self.n, self.me, self.part, self.recv = n, me, part, recv
        self.sems, self.recv_sems, self.device = sems, recv_sems, device
        self.far = n // 2

    def at(self, hops):
        return lax.rem(self.me + hops + self.n, self.n)

    def copy(self, way, step, half, piece):
        return remote(
            self.part(piece, half),
            self.recv.at[way, step, half],
            self.sems.at[0],
            self.recv_sems.at[way, step],
            self.device(self.at(1 if way == 0 else -1)),
        )

    def add(self, way, step, half, piece):
        view = self.part(piece, half)
        view[...] = view[...] + self.recv[way, step, half]

    def first(self):
        for way in range(2):
            self.copy(way, 0, way, self.at(self.far)).start()

    def early(self, way):
        if self.far == 2:
            self.copy(way, 1, 1 - way, self.at(1 if way == 0 else -1)).start()

    def second(self):
        if self.far == 2:
            for way in range(2):
                piece = self.at(1 if way == 0 else -1)
                self.copy(way, 0, way, piece).wait_recv()
                self.add(way, 0, way, piece)
                self.copy(way, 1, way, piece).start()

    def finish(self):
        for way in range(2):
            if self.far == 2:
                view = self.recv.at[way, 1]
                remote(
                    view,
                    view,
                    self.sems.at[0],
                    self.recv_sems.at[way, 1],
                    self.device(self.me),
                ).wait_recv()
                self.add(way, 1, 0, self.me)
                self.add(way, 1, 1, self.me)
            else:
                self.copy(way, 0, way, self.me).wait_recv()
                self.add(way, 0, way, self.me)


def kernel(
    sizes,
    emb_hbm,
    que_hbm,
    pro_hbm,
    pair_hbm,
    out_e,
    out_p,
    out_l,
    emb,
    que,
    pro,
    pair,
    ex,
    sx,
    yx,
    rows_bf,
    part_bf,
    pro_bf,
    emb_t,
    pro_t,
    differ,
    colacc,
    dense,
    softp,
    rbc,
    stb,
    qpart,
    dpbuf,
    xbuf,
    zbuf,
    sxbuf,
    szbuf,
    ldp,
    lx,
    lz,
    pc,
    sib,
    yrecv,
    h1,
    h2,
    x1recv,
    z1recv,
    z2recv,
    x2recv,
    load_sems,
    dp_sems,
    x_sems,
    z_sems,
    soft_sems,
    loss_sems,
    sib_send,
    sib_recv,
    y_sems,
    y_pairs,
    ring_sems,
    x1_sems,
    x1_pairs,
    z1_sems,
    yg_recv,
    zg_recv,
):
    ny, nx, nz = sizes
    dp_count = ny * CORES
    crops, depth = emb.shape
    rows = crops + que.shape[0]
    cols = pro.shape[1]
    total_rows = rows * dp_count
    total_crops = crops * dp_count
    lane_blocks = cols // 128
    row_blocks = rows // 128
    crop_blocks = crops // 128
    width = cols // dp_count
    tile = 256

    my_dp = lax.axis_index("dp")
    my_proto = lax.axis_index("proto")
    my_y, my_c = my_dp // CORES, lax.rem(my_dp, CORES)
    my_z, my_x = my_proto // nx, lax.rem(my_proto, nx)

    def on_dp(index):
        return (index, my_proto)

    def on_x(index):
        return (my_dp, my_z * nx + index)

    def on_z(index):
        return (my_dp, index * nx + my_x)

    def on_y(index):
        return (index * CORES + my_c, my_proto)

    sibling = (my_y * CORES + 1 - my_c, my_proto)

    loads = [
        pltpu.make_async_copy(source, target, load_sems.at[i])
        for i, (source, target) in enumerate(
            ((emb_hbm, emb), (que_hbm, que), (pro_hbm, pro), (pair_hbm, pair))
        )
    ]
    for load in loads:
        load.start()
    barrier = pltpu.get_barrier_semaphore()
    for me, size, device in ((my_z, nz, on_z), (my_x, nx, on_x), (my_dp, dp_count, on_dp)):
        for hop in far_first(size):
            pl.semaphore_signal(
                barrier, inc=1, device_id=device(lax.rem(me + hop, size)), device_id_type=MESH
            )

    loads[0].wait()
    loads[1].wait()

    @pl.loop(0, crops // tile)
    def _(i):
        block = aligned(i, tile)
        for source, first in ((emb, 0), (que, crops)):
            values = source[block, :].astype(F32)
            inv = inv_norm(jnp.sum(values * values, axis=1, keepdims=True))
            start = pl.multiple_of(first + i * tile, tile)
            rows_bf[pl.ds(start, tile), :] = (values * inv).astype(BF16)

    loads[2].wait()
    loads[3].wait()

    @pl.loop(0, cols // tile)
    def _(j):
        block = aligned(j, tile)
        values = pro[:, block].astype(F32)
        inv = inv_norm(jnp.sum(values * values, axis=0, keepdims=True))
        pro_bf[:, block] = (values * inv).astype(BF16)

    wide = colacc.shape[2]
    softp[...] = jnp.zeros_like(softp)

    @pl.loop(0, cols // wide)
    def _(j):
        block = aligned(j, wide)
        weights = pro_bf[:, block]
        acc = jnp.zeros((8, wide), F32)
        for i in range(rows // tile):
            lines = slice(i * tile, (i + 1) * tile)
            scores = jnp.dot(rows_bf[lines, :], weights, preferred_element_type=F32)
            if i < crops // tile:
                sx[lines, block] = scores
                soft = jnp.exp2(scores * (10.0 * LOG2E))
                folded = soft[:, :128]
                for k in range(1, wide // 128):
                    folded = folded + soft[:, k * 128 : (k + 1) * 128]
                softp[lines, :] += folded
                expo = soft * soft
            else:
                expo = jnp.exp2(scores * (20.0 * LOG2E))
            ex[lines, block] = expo
            acc = acc + jnp.sum(expo.reshape(tile // 8, 8, wide), axis=0)
        colacc[j] = acc

    def dense_cols():
        pieces = []
        for j in range(lane_blocks):
            k, part = j * 128 // wide, (j * 128) % wide
            pieces.append(jnp.sum(colacc[k, :, part : part + 128], axis=0, keepdims=True))
        return jnp.concatenate(pieces, axis=0)

    def dense_rows(source, blocks):
        pieces = []
        for b in range(blocks):
            pieces.append(
                jnp.sum(source[b * 128 : (b + 1) * 128, :].T, axis=0, keepdims=True)
            )
        return jnp.concatenate(pieces, axis=0)

    def spread_rows(target, dense, blocks, first=0):
        for b in range(blocks):
            target[(first + b) * 128 : (first + b + 1) * 128, :] = jnp.broadcast_to(
                dense[b : b + 1, :], (128, 128)
            ).T

    def col_pass(first, last, accs):
        groups = 4

        def step(i, accs):
            accs = list(accs)
            for g in range(groups):
                lines = pl.ds(pl.multiple_of(i * 8 * groups + 8 * g, 8), 8)
                scale = rbc[lines, :]
                for j in range(lane_blocks):
                    accs[j] = accs[j] + ex[lines, j * 128 : (j + 1) * 128] * scale
            return tuple(accs)

        return lax.fori_loop(first // (8 * groups), last // (8 * groups), step, accs)

    def spread_cols(dense):
        return [
            jnp.broadcast_to(dense[j : j + 1, :], (8, 128)) for j in range(lane_blocks)
        ]

    def row_sums(target, start, count, line_sums):
        pair = 2

        @pl.loop(start // (128 * pair), (start + count) // (128 * pair))
        def _(i):
            for k in range(pair):
                first = (i * pair + k) * 128
                accs = [
                    line_sums(pl.ds(pl.multiple_of(first + 8 * g, 8), 8)) for g in range(16)
                ]
                turned = jnp.concatenate(accs, axis=0).T
                target[pl.ds(i * pair + k, 1), :] = jnp.sum(turned, axis=0, keepdims=True)

    def row_pass(scales, start, count):
        def line_sums(lines):
            acc = ex[lines, :128] * scales[0]
            for j in range(1, lane_blocks):
                acc = acc + ex[lines, j * 128 : (j + 1) * 128] * scales[j]
            return acc

        row_sums(dense, start, count, line_sums)

    def partner_pass(scales):
        def line_sums(lines):
            acc = jnp.zeros((8, 128), F32)
            for j in range(lane_blocks):
                block = slice(j * 128, (j + 1) * 128)
                code = yx[lines, block] * scales[j]
                yx[lines, block] = code
                acc = acc + code
            return acc

        row_sums(dense, 0, crops, line_sums)

    def soften(first, last):
        groups = 2

        @pl.loop(first // (8 * groups), last // (8 * groups))
        def _(i):
            for g in range(groups):
                lines = pl.ds(pl.multiple_of(i * 8 * groups + 8 * g, 8), 8)
                scale = stb[lines, :]
                acc = jnp.zeros((8, 128), F32)
                for j in range(lane_blocks):
                    block = slice(j * 128, (j + 1) * 128)
                    score = sx[lines, block]
                    acc = acc + yx[lines, block] * score
                    sx[lines, block] = jnp.exp2(score * (10.0 * LOG2E)) * scale
                qpart[lines, :] = acc

    def pick_partners():
        local_pair = pair[...] - my_dp * crops

        @pl.loop(0, crops // tile)
        def _(i):
            block = aligned(i, tile)
            line = lax.broadcasted_iota(jnp.int32, (tile, crops), 0) + i * tile
            pick = jnp.where(line == local_pair, 1.0, 0.0).astype(BF16)
            part_bf[block, :] = jnp.dot(
                pick, rows_bf[:crops, :], preferred_element_type=F32
            ).astype(BF16)

    def partner_exponents():
        @pl.loop(0, cols // tile)
        def _(j):
            block = aligned(j, tile)
            weights = pro_bf[:, block]
            for i in range(crops // tile):
                lines = slice(i * tile, (i + 1) * tile)
                scores = jnp.dot(part_bf[lines, :], weights, preferred_element_type=F32)
                soft = jnp.exp2(scores * (10.0 * LOG2E))
                yx[lines, block] = soft * soft

    def transposed_rows():
        @pl.loop(0, crops // tile)
        def _(i):
            block = aligned(i, tile)
            emb_t[:, block] = rows_bf[block, :].astype(F32).T.astype(BF16)

    def transposed_cols():
        @pl.loop(0, cols // tile)
        def _(j):
            block = aligned(j, tile)
            pro_t[block, :] = pro_bf[:, block].astype(F32).T.astype(BF16)

    pl.semaphore_wait(barrier, dp_count - 1 + nx - 1 + nz - 1)
    col_dense = dense_cols()
    soft_total = None
    row_sum = None
    soft_x = Exchange(sxbuf, soft_sems.at[0], my_x, nx, on_x)
    soft_z = Exchange(szbuf, soft_sems.at[1], my_z, nz, on_z)
    half_blocks = row_blocks // 2
    for it in range(ITERS):
        over_dp = Exchange(dpbuf.at[it], dp_sems.at[it], my_dp, dp_count, on_dp)
        over_x = [
            Exchange(
                xbuf.at[it, :, pl.ds(h * half_blocks, half_blocks)],
                x_sems.at[it, h],
                my_x,
                nx,
                on_x,
            )
            for h in range(2)
        ]
        over_z = [
            Exchange(
                zbuf.at[it, :, pl.ds(h * half_blocks, half_blocks)],
                z_sems.at[it, h],
                my_z,
                nz,
                on_z,
            )
            for h in range(2)
        ]
        over_dp.start(col_dense)
        if it == 0:
            pick_partners()
            soft_part = dense_rows(softp, crop_blocks)
        elif it == 1:
            soft_x.start(soft_part)
            transposed_cols()
        else:
            soft_total = soft_z.finish()
            spread_rows(stb, 10.0 / soft_total, crop_blocks)
        col_scale = 1.0 / (PROTOS * over_dp.finish())
        if it < ITERS - 1:
            scales = spread_cols(col_scale)
            for h in range(2):
                row_pass(scales, h * (rows // 2), rows // 2)
                over_x[h].start(dense[h * half_blocks : (h + 1) * half_blocks, :])
            if it == 0:
                transposed_rows()
            else:
                soft_z.start(soft_x.finish())
            for h in range(2):
                over_z[h].start(over_x[h].finish())
            if it == 0:
                partner_exponents()
            accs = (jnp.zeros((8, 128), F32),) * lane_blocks
            for h in range(2):
                scale = 1.0 / (total_rows * over_z[h].finish())
                spread_rows(rbc, scale, half_blocks, h * half_blocks)
                accs = col_pass(h * (rows // 2), (h + 1) * (rows // 2), accs)
            col_dense = jnp.concatenate(
                [jnp.sum(a, axis=0, keepdims=True) for a in accs], axis=0
            )
        else:
            partner_pass(spread_cols(10.0 * col_scale))
            over_x[0].start(dense[:crop_blocks, :])
            soften(0, crops // 2)
            over_z[0].start(over_x[0].finish())
            soften(crops // 2, crops)
            row_sum = over_z[0].finish()

    spread_rows(rbc, 10.0 / row_sum, crop_blocks)

    share = crops // (nx * nz)
    rest = share // 4
    groups = 3
    first_share = groups * rest
    x_line = nz * share

    def x_ring(g):
        return Ring(
            nx,
            my_x,
            lambda t, half: h1.at[g, t, pl.ds(half * (nz // 2), nz // 2)],
            x1recv.at[g],
            x1_sems.at[g],
            x1_pairs.at[g],
            on_x,
        )

    def z_scatter(g):
        return Scatter(nz, my_z, lambda t: h1.at[g, my_x, t], z1recv.at[g], z1_sems.at[g], on_z)

    x1 = [x_ring(g) for g in range(groups)]
    z1 = [z_scatter(g) for g in range(groups)]
    z2 = Scatter(nz, my_z, lambda t: h2.at[t], z2recv, ring_sems.at[2], on_z)
    x2 = Scatter(nx, my_x, lambda t: h2.at[my_z, t], x2recv, ring_sems.at[3], on_x)

    repeat = tile // 128
    for hops in [nx // 2] + ([1, -1] if nx == 4 else []) + [0]:
        t = x1[0].at(hops)
        lines = aligned(t, x_line)
        scale = jnp.concatenate([rbc[lines, :]] * repeat, axis=1)
        for j in range(cols // tile):
            block = slice(j * tile, (j + 1) * tile)
            value = sx[lines, block] - yx[lines, block] * scale
            differ[lines, block] = value.astype(BF16)
        cot = jnp.dot(differ[lines, :], pro_t[...], preferred_element_type=F32)
        for pz in range(nz):
            for g in range(groups):
                first = pz * share + g * rest
                h1[g, t, pz] = cot[first : first + rest, :]
            h2[pz, t] = cot[pz * share + first_share : (pz + 1) * share, :]
        for ring in x1:
            if hops == nx // 2:
                ring.first()
            elif hops == 1:
                ring.early(0)
            elif hops == -1:
                ring.early(1)
    z2.start()

    half_depth = depth // 2
    parts = 2
    narrow = width // parts

    def piece(t, core):
        block = aligned(t * CORES + core, width)
        cot = jnp.dot(emb_t[...], differ[:, block], preferred_element_type=F32)
        for part in range(parts):
            across = slice(part * narrow, (part + 1) * narrow)
            pc[part, t, core, 0] = cot[:half_depth, across]
            pc[part, t, core, 1] = cot[half_depth:, across]

    def to_sibling(number, t):
        return remote(
            pc.at[:, t, 1 - my_c], sib.at[number], sib_send.at[0], sib_recv.at[number], sibling
        )

    def y_ring_of(part):
        return Ring(
            ny,
            my_y,
            lambda t, half: pc.at[part, t, my_c, half],
            yrecv.at[part],
            y_sems.at[part],
            y_pairs.at[part],
            on_y,
        )

    y_rings = [y_ring_of(part) for part in range(parts)]
    y_at = y_rings[0].at
    near = [1, -1] if ny == 4 else []
    order = [ny // 2] + near + [0]
    for number, hops in enumerate(order):
        t = y_at(hops)
        piece(t, 1 - my_c)
        to_sibling(number, t).start()
        piece(t, my_c)
        to_sibling(number, t).wait_recv()
        for part in range(parts):
            pc[part, t, my_c] = pc[part, t, my_c] + sib[number, part]
        if hops == ny // 2:
            y_rings[0].first()
        elif hops == 1:
            y_rings[0].early(0)
        elif hops == -1:
            y_rings[0].early(1)
    y_rings[1].first()

    def add_up(i, acc):
        lines = aligned(i, 8)
        return acc + qpart[lines, :] * rbc[lines, :]

    code_score = lax.fori_loop(0, crops // 8, add_up, jnp.zeros((8, 128), F32))
    log_total = jnp.log(soft_total) * (1.0 / (nx * nz))
    if crop_blocks != 8:
        log_total = jnp.broadcast_to(jnp.sum(log_total, axis=0, keepdims=True), (8, 128)) / 8.0
    loss_dp = Exchange(ldp, loss_sems.at[0], my_dp, dp_count, on_dp)
    loss_x = Exchange(lx, loss_sems.at[1], my_x, nx, on_x)
    loss_z = Exchange(lz, loss_sems.at[2], my_z, nz, on_z)
    loss_dp.start(log_total - code_score)

    for ring in x1:
        ring.second()
    y_rings[0].second()
    y_rings[1].early(0)
    y_rings[1].early(1)
    for ring, scatter in zip(x1, z1):
        ring.finish()
        scatter.start()
        if ring is x1[0]:
            y_rings[1].second()
    h2[my_z] = z2.finish()
    x2.start()

    def columns(t, core, part):
        first = (t * CORES + core) * width + part * narrow
        return pl.ds(pl.multiple_of(first, narrow), narrow)

    def pull_columns(part):
        block = columns(my_y, my_c, part)
        values = pro[:, block].astype(F32)
        inv = inv_norm(jnp.sum(values * values, axis=0, keepdims=True))
        cots = [pc[part, my_y, my_c, 0], pc[part, my_y, my_c, 1]]
        along = jnp.sum(cots[0] * values[:half_depth, :], axis=0, keepdims=True) + jnp.sum(
            cots[1] * values[half_depth:, :], axis=0, keepdims=True
        )
        factor = PROTOS / math.sqrt(total_crops)
        pull = along * (inv * inv * inv) * factor
        scale = inv * factor
        out_p[0, :, block] = cots[0] * scale - values[:half_depth, :] * pull
        out_p[1, :, block] = cots[1] * scale - values[half_depth:, :] * pull

    def along_y(way, step, half, t, part):
        view = out_p.at[half, :, columns(t, my_c, part)]
        peer = on_y(y_at(1 if way == 0 else -1))
        return remote(view, view, ring_sems.at[5, 0], yg_recv.at[part, way, step, half], peer)

    def hand_on(t, part):
        view = out_p.at[:, :, columns(t, my_c, part)]
        remote(view, view, ring_sems.at[6, 0], ring_sems.at[6, 1], sibling).start()

    def give_y(part):
        y_rings[part].finish()
        pull_columns(part)
        if ny == 4:
            for half in range(2):
                along_y(0, 0, half, my_y, part).start()
                along_y(1, 0, 1 - half, my_y, part).start()
        else:
            along_y(0, 1, 0, my_y, part).start()
            along_y(1, 1, 1, my_y, part).start()
        hand_on(my_y, part)

    give_y(0)

    def pull_rows(cot, first, count):
        values = emb[aligned(my_x * nz + my_z, share), :].astype(F32)
        values = values[first : first + count, :]
        inv = inv_norm(jnp.sum(values * values, axis=1, keepdims=True))
        along = jnp.sum(cot * values, axis=1, keepdims=True)
        factor = math.sqrt(PROTOS)
        out_e[my_x, my_z, pl.ds(first, count)] = cot * (inv * factor) - values * (
            along * (inv * inv * inv) * factor
        )

    late = pl.ds(first_share, rest)
    soon = pl.ds(0, first_share)

    def z_at(hops):
        return lax.rem(my_z + hops + nz, nz)

    def over_x_from(rel):
        view = out_e.at[my_x, z_at(rel), soon]
        for hop in far_first(nx):
            remote(
                view, view, ring_sems.at[1, 0], ring_sems.at[1, 1], on_x(x1[0].at(hop))
            ).start()

    def over_z_at(rel):
        view = out_e.at[my_x, my_z, soon]
        return remote(view, view, ring_sems.at[4, 0], zg_recv.at[rel], on_z(z_at(rel)))

    pull_rows(x2.finish(), first_share, rest)
    for hop in far_first(nx):
        view = out_e.at[my_x, my_z, late]
        remote(
            view, view, ring_sems.at[7, 0], ring_sems.at[7, 1], on_x(x1[0].at(hop))
        ).start()
    give_y(1)
    pull_rows(jnp.concatenate([scatter.finish() for scatter in z1], axis=0), 0, first_share)
    for hop in far_first(nz):
        over_z_at(hop).start()
    over_x_from(0)

    loss_x.start(loss_dp.finish())

    def receive_z(rel):
        view = out_e.at[my_x, z_at(rel), soon]
        remote(view, view, ring_sems.at[4, 0], zg_recv.at[nz - rel], on_z(my_z)).wait_recv()
        over_x_from(rel)

    def send_late():
        arrived(out_e.at[pl.ds(0, nx - 1), 0, late], ring_sems.at[7], on_x(my_x))
        for hop in far_first(nz):
            view = out_e.at[:, my_z, late]
            remote(
                view, view, ring_sems.at[0, 0], ring_sems.at[0, 1], on_z(z_at(hop))
            ).start()

    def receive_y(way, step, half, part):
        t = y_at((-1 if way == 0 else 1) if step == 0 else ny // 2)
        view = out_p.at[half, :, columns(t, my_c, part)]
        remote(
            view, view, ring_sems.at[5, 0], yg_recv.at[part, way, step, half], on_y(my_y)
        ).wait_recv()

    def near_y(part, first):
        if ny == 4:
            for way in range(2):
                half = way if first else 1 - way
                t = y_at(-1 if way == 0 else 1)
                receive_y(way, 0, half, part)
                if first:
                    along_y(way, 1, half, t, part).start()
                else:
                    hand_on(t, part)

    pending = [nz - hop for hop in far_first(nz)]
    near_y(0, True)
    near_y(1, True)
    send_late()
    for rel in pending:
        receive_z(rel)
    near_y(0, False)
    loss_z.start(loss_x.finish())
    near_y(1, False)
    for part in range(parts):
        for way in range(2):
            receive_y(way, 1, way, part)
        hand_on(y_at(ny // 2), part)
    out_l[0, 0] = jnp.sum(loss_z.finish()) / total_crops

    arrived(out_e.at[:, pl.ds(0, nz - 1), late], ring_sems.at[0], on_z(my_z))
    arrived(out_e.at[pl.ds(0, nx - 1), :, soon], ring_sems.at[1], on_x(my_x))
    own = out_p.at[:, :, pl.ds(0, ny * width)]
    arrived(own, ring_sems.at[6], sibling)
    departed(own, ring_sems.at[6], sibling)
    for g in range(groups):
        departed(h1.at[g, pl.ds(0, nx - 1)], x1_sems.at[g], on_x(my_x))
    for ring in (*z1, z2, x2):
        ring.close()
    for part in range(parts):
        departed(pc.at[part, pl.ds(0, ny - 1), 0], y_sems.at[part], on_y(my_y))
    remote(pc.at[:, :, 0], pc.at[:, :, 0], sib_send.at[0], sib_recv.at[0], sibling).wait_send()
    departed(out_p.at[:, :, pl.ds(0, (ny - 1) * width)], ring_sems.at[5], on_y(my_y))
    departed(out_e.at[pl.ds(0, nx - 1), 0, late], ring_sems.at[7], on_x(my_x))
    departed(out_e.at[0, pl.ds(0, nz - 1), soon], ring_sems.at[4], on_z(my_z))
    departed(out_e.at[pl.ds(0, nx - 1), :, soon], ring_sems.at[1], on_x(my_x))
    departed(out_e.at[:, pl.ds(0, nz - 1), late], ring_sems.at[0], on_z(my_z))


def local(sizes, embeddings, queue, prototypes, pairing):
    ny, nx, nz = sizes
    dp_count = ny * CORES
    crops, depth = embeddings.shape
    rows = crops + queue.shape[0]
    cols = prototypes.shape[1]
    width = cols // dp_count
    share = crops // (nx * nz)
    rest = share // 4
    row_blocks, crop_blocks, lane_blocks = rows // 128, crops // 128, cols // 128
    half = depth // 2
    tile = 256
    dma = pltpu.SemaphoreType.DMA
    vmem = pltpu.VMEM
    scratch = [
        vmem((crops, depth), BF16),
        vmem((rows - crops, depth), BF16),
        vmem((depth, cols), BF16),
        vmem((1, crops), jnp.int32),
        vmem((rows, cols), F32),
        vmem((crops, cols), F32),
        vmem((crops, cols), F32),
        vmem((rows, depth), BF16),
        vmem((crops, depth), BF16),
        vmem((depth, cols), BF16),
        vmem((depth, crops), BF16),
        vmem((cols, depth), BF16),
        vmem((crops, cols), BF16),
        vmem((cols // 512, 8, 512), F32),
        vmem((row_blocks, 128), F32),
        vmem((crops, 128), F32),
        vmem((rows, 128), F32),
        vmem((crops, 128), F32),
        vmem((crops, 128), F32),
        vmem((ITERS, dp_count, lane_blocks, 128), F32),
        vmem((ITERS, nx, row_blocks, 128), F32),
        vmem((ITERS, nz, row_blocks, 128), F32),
        vmem((nx, crop_blocks, 128), F32),
        vmem((nz, crop_blocks, 128), F32),
        vmem((dp_count, 8, 128), F32),
        vmem((nx, 8, 128), F32),
        vmem((nz, 8, 128), F32),
        vmem((2, ny, CORES, 2, half, width // 2), F32),
        vmem((ny, 2, 2, half, width // 2), F32),
        vmem((2, 2, 2, 2, half, width // 2), F32),
        vmem((3, nx, nz, rest, depth), F32),
        vmem((nz, nx, rest, depth), F32),
        vmem((3, 2, 2, 2, nz // 2, rest, depth), F32),
        vmem((3, nz - 1, rest, depth), F32),
        vmem((nz - 1, nx, rest, depth), F32),
        vmem((nx - 1, rest, depth), F32),
        dma((4,)),
        dma((ITERS, 2)),
        dma((ITERS, 2, 2)),
        dma((ITERS, 2, 2)),
        dma((2, 2)),
        dma((3, 2)),
        dma((1,)),
        dma((ny,)),
        dma((2, 2)),
        dma((2, 2, 2)),
        dma((8, 2)),
        dma((3, 2)),
        dma((3, 2, 2)),
        dma((3, 2)),
        dma((2, 2, 2, 2)),
        dma((nz,)),
    ]
    in_vmem = pl.BlockSpec(memory_space=pltpu.VMEM)
    anywhere = pl.BlockSpec(memory_space=pl.ANY)
    grad_embed, grad_proto, loss = pl.pallas_call(
        functools.partial(kernel, sizes),
        out_shape=(
            pltpu.VMEM((nx, nz, share, depth), F32),
            pltpu.VMEM((2, half, cols), F32),
            jax.ShapeDtypeStruct((1, 1), F32),
        ),
        in_specs=[anywhere] * 4,
        out_specs=(in_vmem, in_vmem, pl.BlockSpec(memory_space=pltpu.SMEM)),
        scratch_shapes=scratch,
        compiler_params=pltpu.CompilerParams(
            collective_id=0, has_side_effects=True, vmem_limit_bytes=59 * 1024 * 1024
        ),
    )(embeddings, queue, prototypes, pairing.reshape(1, crops))
    return (
        grad_embed.reshape(crops, depth),
        grad_proto.reshape(depth, cols),
        loss.reshape(()),
    )


def solution(mesh):
    nx = ALONG_X
    sizes = (mesh.shape["dp"] // CORES, nx, mesh.shape["proto"] // nx)
    return jax.shard_map(
        functools.partial(local, sizes),
        mesh=mesh,
        in_specs=(P("dp", None), P("dp", None), P(None, "proto"), P("dp")),
        out_specs=(P("dp", None), P(None, "proto"), P()),
        check_vma=False,
    )
```

```python
import functools
import math

import jax
import jax.numpy as jnp
from jax import lax
from jax.experimental import pallas as pl
from jax.experimental.pallas import tpu as pltpu
from jax.sharding import PartitionSpec as P

PROTOS = 65536
ITERS = 3
CORES = 2
ALONG_X = 4
LOG2E = math.log2(math.e)
F32 = jnp.float32
BF16 = jnp.bfloat16
MESH = pl.DeviceIdType.MESH


def inv_norm(sum_sq):
    shifted = sum_sq + 1e-06
    guess = lax.rsqrt(shifted)
    return guess * (1.5 - 0.5 * shifted * guess * guess)


def aligned(index, size):
    return pl.ds(pl.multiple_of(index * size, size), size)


def remote(src, dst, send_sem, recv_sem, device):
    return pltpu.make_async_remote_copy(
        src_ref=src,
        dst_ref=dst,
        send_sem=send_sem,
        recv_sem=recv_sem,
        device_id=device,
        device_id_type=MESH,
    )


def arrived(view, sems, device):
    remote(view, view, sems.at[0], sems.at[1], device).wait_recv()


def departed(view, sems, device):
    remote(view, view, sems.at[0], sems.at[1], device).wait_send()


def far_first(size):
    return sorted(range(1, size), key=lambda hop: (-min(hop, size - hop), hop))


class Exchange:
    def __init__(self, buf, sems, me, size, device):
        self.buf, self.sems, self.me, self.size, self.device = buf, sems, me, size, device

    def start(self, block):
        self.buf[self.me] = block
        for hop in far_first(self.size):
            slot = self.buf.at[self.me]
            peer = self.device(lax.rem(self.me + hop, self.size))
            remote(slot, slot, self.sems.at[0], self.sems.at[1], peer).start()

    def finish(self):
        others = self.buf.at[pl.ds(0, self.size - 1)]
        arrived(others, self.sems, self.device(self.me))
        departed(others, self.sems, self.device(self.me))
        total = self.buf[0]
        for slot in range(1, self.size):
            total = total + self.buf[slot]
        return total


class Scatter:
    def __init__(self, n, me, part, recv, sems, device):
        self.n, self.me, self.part, self.recv = n, me, part, recv
        self.sems, self.device = sems, device

    def start(self):
        for hop in far_first(self.n):
            piece = lax.rem(self.me + hop, self.n)
            remote(
                self.part(piece),
                self.recv.at[hop - 1],
                self.sems.at[0],
                self.sems.at[1],
                self.device(piece),
            ).start()

    def finish(self):
        arrived(self.recv, self.sems, self.device(self.me))
        total = self.part(self.me)[...]
        for hop in range(1, self.n):
            total = total + self.recv[hop - 1]
        return total

    def close(self):
        departed(self.recv, self.sems, self.device(self.me))


class Ring:
    def __init__(self, n, me, part, recv, sems, recv_sems, device):
        self.n, self.me, self.part, self.recv = n, me, part, recv
        self.sems, self.recv_sems, self.device = sems, recv_sems, device
        self.far = n // 2

    def at(self, hops):
        return lax.rem(self.me + hops + self.n, self.n)

    def copy(self, way, step, half, piece):
        return remote(
            self.part(piece, half),
            self.recv.at[way, step, half],
            self.sems.at[0],
            self.recv_sems.at[way, step],
            self.device(self.at(1 if way == 0 else -1)),
        )

    def add(self, way, step, half, piece):
        view = self.part(piece, half)
        view[...] = view[...] + self.recv[way, step, half]

    def first(self):
        for way in range(2):
            self.copy(way, 0, way, self.at(self.far)).start()

    def early(self, way):
        if self.far == 2:
            self.copy(way, 1, 1 - way, self.at(1 if way == 0 else -1)).start()

    def second(self):
        if self.far == 2:
            for way in range(2):
                piece = self.at(1 if way == 0 else -1)
                self.copy(way, 0, way, piece).wait_recv()
                self.add(way, 0, way, piece)
                self.copy(way, 1, way, piece).start()

    def finish(self):
        for way in range(2):
            if self.far == 2:
                view = self.recv.at[way, 1]
                remote(
                    view,
                    view,
                    self.sems.at[0],
                    self.recv_sems.at[way, 1],
                    self.device(self.me),
                ).wait_recv()
                self.add(way, 1, 0, self.me)
                self.add(way, 1, 1, self.me)
            else:
                self.copy(way, 0, way, self.me).wait_recv()
                self.add(way, 0, way, self.me)


def kernel(
    sizes,
    emb_hbm,
    que_hbm,
    pro_hbm,
    pair_hbm,
    out_e,
    out_p,
    out_l,
    emb,
    que,
    pro,
    pair,
    ex,
    sx,
    yx,
    rows_bf,
    part_bf,
    pro_bf,
    emb_t,
    pro_t,
    differ,
    colacc,
    dense,
    softp,
    rbc,
    stb,
    qpart,
    dpbuf,
    xbuf,
    zbuf,
    sxbuf,
    szbuf,
    ldp,
    lx,
    lz,
    pc,
    sib,
    yrecv,
    h1,
    h2,
    x1recv,
    z1recv,
    z2recv,
    x2recv,
    load_sems,
    dp_sems,
    x_sems,
    z_sems,
    soft_sems,
    loss_sems,
    sib_send,
    sib_recv,
    y_sems,
    y_pairs,
    ring_sems,
    x1_sems,
    x1_pairs,
    z1_sems,
    yg_recv,
    zg_recv,
):
    ny, nx, nz = sizes
    dp_count = ny * CORES
    crops, depth = emb.shape
    rows = crops + que.shape[0]
    cols = pro.shape[1]
    total_rows = rows * dp_count
    total_crops = crops * dp_count
    lane_blocks = cols // 128
    row_blocks = rows // 128
    crop_blocks = crops // 128
    width = cols // dp_count
    tile = 256

    my_dp = lax.axis_index("dp")
    my_proto = lax.axis_index("proto")
    my_y, my_c = my_dp // CORES, lax.rem(my_dp, CORES)
    my_z, my_x = my_proto // nx, lax.rem(my_proto, nx)

    def on_dp(index):
        return (index, my_proto)

    def on_x(index):
        return (my_dp, my_z * nx + index)

    def on_z(index):
        return (my_dp, index * nx + my_x)

    def on_y(index):
        return (index * CORES + my_c, my_proto)

    sibling = (my_y * CORES + 1 - my_c, my_proto)

    loads = [
        pltpu.make_async_copy(source, target, load_sems.at[i])
        for i, (source, target) in enumerate(
            ((emb_hbm, emb), (que_hbm, que), (pro_hbm, pro), (pair_hbm, pair))
        )
    ]
    for load in loads:
        load.start()
    barrier = pltpu.get_barrier_semaphore()
    for me, size, device in ((my_z, nz, on_z), (my_x, nx, on_x), (my_dp, dp_count, on_dp)):
        for hop in far_first(size):
            pl.semaphore_signal(
                barrier, inc=1, device_id=device(lax.rem(me + hop, size)), device_id_type=MESH
            )

    loads[0].wait()
    loads[1].wait()

    @pl.loop(0, crops // tile)
    def _(i):
        block = aligned(i, tile)
        for source, first in ((emb, 0), (que, crops)):
            values = source[block, :].astype(F32)
            inv = inv_norm(jnp.sum(values * values, axis=1, keepdims=True))
            start = pl.multiple_of(first + i * tile, tile)
            rows_bf[pl.ds(start, tile), :] = (values * inv).astype(BF16)

    loads[2].wait()
    loads[3].wait()

    @pl.loop(0, cols // tile)
    def _(j):
        block = aligned(j, tile)
        values = pro[:, block].astype(F32)
        inv = inv_norm(jnp.sum(values * values, axis=0, keepdims=True))
        pro_bf[:, block] = (values * inv).astype(BF16)

    wide = colacc.shape[2]
    softp[...] = jnp.zeros_like(softp)

    @pl.loop(0, cols // wide)
    def _(j):
        block = aligned(j, wide)
        weights = pro_bf[:, block]
        acc = jnp.zeros((8, wide), F32)
        for i in range(rows // tile):
            lines = slice(i * tile, (i + 1) * tile)
            scores = jnp.dot(rows_bf[lines, :], weights, preferred_element_type=F32)
            if i < crops // tile:
                sx[lines, block] = scores
                soft = jnp.exp2(scores * (10.0 * LOG2E))
                folded = soft[:, :128]
                for k in range(1, wide // 128):
                    folded = folded + soft[:, k * 128 : (k + 1) * 128]
                softp[lines, :] += folded
                expo = soft * soft
            else:
                expo = jnp.exp2(scores * (20.0 * LOG2E))
            ex[lines, block] = expo
            acc = acc + jnp.sum(expo.reshape(tile // 8, 8, wide), axis=0)
        colacc[j] = acc

    def dense_cols():
        pieces = []
        for j in range(lane_blocks):
            k, part = j * 128 // wide, (j * 128) % wide
            pieces.append(jnp.sum(colacc[k, :, part : part + 128], axis=0, keepdims=True))
        return jnp.concatenate(pieces, axis=0)

    def dense_rows(source, blocks):
        pieces = []
        for b in range(blocks):
            pieces.append(
                jnp.sum(source[b * 128 : (b + 1) * 128, :].T, axis=0, keepdims=True)
            )
        return jnp.concatenate(pieces, axis=0)

    def spread_rows(target, dense, blocks, first=0):
        for b in range(blocks):
            target[(first + b) * 128 : (first + b + 1) * 128, :] = jnp.broadcast_to(
                dense[b : b + 1, :], (128, 128)
            ).T

    def col_pass(first, last, accs):
        groups = 4

        def step(i, accs):
            accs = list(accs)
            for g in range(groups):
                lines = pl.ds(pl.multiple_of(i * 8 * groups + 8 * g, 8), 8)
                scale = rbc[lines, :]
                for j in range(lane_blocks):
                    accs[j] = accs[j] + ex[lines, j * 128 : (j + 1) * 128] * scale
            return tuple(accs)

        return lax.fori_loop(first // (8 * groups), last // (8 * groups), step, accs)

    def spread_cols(dense):
        return [
            jnp.broadcast_to(dense[j : j + 1, :], (8, 128)) for j in range(lane_blocks)
        ]

    def row_sums(target, start, count, line_sums):
        pair = 2

        @pl.loop(start // (128 * pair), (start + count) // (128 * pair))
        def _(i):
            for k in range(pair):
                first = (i * pair + k) * 128
                accs = [
                    line_sums(pl.ds(pl.multiple_of(first + 8 * g, 8), 8)) for g in range(16)
                ]
                turned = jnp.concatenate(accs, axis=0).T
                target[pl.ds(i * pair + k, 1), :] = jnp.sum(turned, axis=0, keepdims=True)

    def row_pass(scales, start, count):
        def line_sums(lines):
            acc = ex[lines, :128] * scales[0]
            for j in range(1, lane_blocks):
                acc = acc + ex[lines, j * 128 : (j + 1) * 128] * scales[j]
            return acc

        row_sums(dense, start, count, line_sums)

    def partner_pass(scales):
        def line_sums(lines):
            acc = jnp.zeros((8, 128), F32)
            for j in range(lane_blocks):
                block = slice(j * 128, (j + 1) * 128)
                code = yx[lines, block] * scales[j]
                yx[lines, block] = code
                acc = acc + code
            return acc

        row_sums(dense, 0, crops, line_sums)

    def soften(first, last):
        groups = 2

        @pl.loop(first // (8 * groups), last // (8 * groups))
        def _(i):
            for g in range(groups):
                lines = pl.ds(pl.multiple_of(i * 8 * groups + 8 * g, 8), 8)
                scale = stb[lines, :]
                acc = jnp.zeros((8, 128), F32)
                for j in range(lane_blocks):
                    block = slice(j * 128, (j + 1) * 128)
                    score = sx[lines, block]
                    acc = acc + yx[lines, block] * score
                    sx[lines, block] = jnp.exp2(score * (10.0 * LOG2E)) * scale
                qpart[lines, :] = acc

    def pick_partners():
        local_pair = pair[...] - my_dp * crops

        @pl.loop(0, crops // tile)
        def _(i):
            block = aligned(i, tile)
            line = lax.broadcasted_iota(jnp.int32, (tile, crops), 0) + i * tile
            pick = jnp.where(line == local_pair, 1.0, 0.0).astype(BF16)
            part_bf[block, :] = jnp.dot(
                pick, rows_bf[:crops, :], preferred_element_type=F32
            ).astype(BF16)

    def partner_exponents():
        @pl.loop(0, cols // tile)
        def _(j):
            block = aligned(j, tile)
            weights = pro_bf[:, block]
            for i in range(crops // tile):
                lines = slice(i * tile, (i + 1) * tile)
                scores = jnp.dot(part_bf[lines, :], weights, preferred_element_type=F32)
                soft = jnp.exp2(scores * (10.0 * LOG2E))
                yx[lines, block] = soft * soft

    def transposed_rows():
        @pl.loop(0, crops // tile)
        def _(i):
            block = aligned(i, tile)
            emb_t[:, block] = rows_bf[block, :].astype(F32).T.astype(BF16)

    def transposed_cols():
        @pl.loop(0, cols // tile)
        def _(j):
            block = aligned(j, tile)
            pro_t[block, :] = pro_bf[:, block].astype(F32).T.astype(BF16)

    pl.semaphore_wait(barrier, dp_count - 1 + nx - 1 + nz - 1)
    col_dense = dense_cols()
    soft_total = None
    row_sum = None
    soft_x = Exchange(sxbuf, soft_sems.at[0], my_x, nx, on_x)
    soft_z = Exchange(szbuf, soft_sems.at[1], my_z, nz, on_z)
    half_blocks = row_blocks // 2
    for it in range(ITERS):
        over_dp = Exchange(dpbuf.at[it], dp_sems.at[it], my_dp, dp_count, on_dp)
        over_x = [
            Exchange(
                xbuf.at[it, :, pl.ds(h * half_blocks, half_blocks)],
                x_sems.at[it, h],
                my_x,
                nx,
                on_x,
            )
            for h in range(2)
        ]
        over_z = [
            Exchange(
                zbuf.at[it, :, pl.ds(h * half_blocks, half_blocks)],
                z_sems.at[it, h],
                my_z,
                nz,
                on_z,
            )
            for h in range(2)
        ]
        over_dp.start(col_dense)
        if it == 0:
            pick_partners()
            soft_part = dense_rows(softp, crop_blocks)
        elif it == 1:
            soft_x.start(soft_part)
            transposed_cols()
        else:
            soft_total = soft_z.finish()
            spread_rows(stb, 10.0 / soft_total, crop_blocks)
        col_scale = 1.0 / (PROTOS * over_dp.finish())
        if it < ITERS - 1:
            scales = spread_cols(col_scale)
            for h in range(2):
                row_pass(scales, h * (rows // 2), rows // 2)
                over_x[h].start(dense[h * half_blocks : (h + 1) * half_blocks, :])
            if it == 0:
                transposed_rows()
            else:
                soft_z.start(soft_x.finish())
            for h in range(2):
                over_z[h].start(over_x[h].finish())
            if it == 0:
                partner_exponents()
            accs = (jnp.zeros((8, 128), F32),) * lane_blocks
            for h in range(2):
                scale = 1.0 / (total_rows * over_z[h].finish())
                spread_rows(rbc, scale, half_blocks, h * half_blocks)
                accs = col_pass(h * (rows // 2), (h + 1) * (rows // 2), accs)
            col_dense = jnp.concatenate(
                [jnp.sum(a, axis=0, keepdims=True) for a in accs], axis=0
            )
        else:
            partner_pass(spread_cols(10.0 * col_scale))
            over_x[0].start(dense[:crop_blocks, :])
            soften(0, crops // 2)
            over_z[0].start(over_x[0].finish())
            soften(crops // 2, crops)
            row_sum = over_z[0].finish()

    spread_rows(rbc, 10.0 / row_sum, crop_blocks)

    share = crops // (nx * nz)
    rest = share // 4
    groups = 3
    first_share = groups * rest
    x_line = nz * share

    def x_ring(g):
        return Ring(
            nx,
            my_x,
            lambda t, half: h1.at[g, t, pl.ds(half * (nz // 2), nz // 2)],
            x1recv.at[g],
            x1_sems.at[g],
            x1_pairs.at[g],
            on_x,
        )

    def z_scatter(g):
        return Scatter(nz, my_z, lambda t: h1.at[g, my_x, t], z1recv.at[g], z1_sems.at[g], on_z)

    x1 = [x_ring(g) for g in range(groups)]
    z1 = [z_scatter(g) for g in range(groups)]
    z2 = Scatter(nz, my_z, lambda t: h2.at[t], z2recv, ring_sems.at[2], on_z)
    x2 = Scatter(nx, my_x, lambda t: h2.at[my_z, t], x2recv, ring_sems.at[3], on_x)

    repeat = tile // 128
    for hops in [nx // 2] + ([1, -1] if nx == 4 else []) + [0]:
        t = x1[0].at(hops)
        lines = aligned(t, x_line)
        scale = jnp.concatenate([rbc[lines, :]] * repeat, axis=1)
        for j in range(cols // tile):
            block = slice(j * tile, (j + 1) * tile)
            value = sx[lines, block] - yx[lines, block] * scale
            differ[lines, block] = value.astype(BF16)
        cot = jnp.dot(differ[lines, :], pro_t[...], preferred_element_type=F32)
        for pz in range(nz):
            for g in range(groups):
                first = pz * share + g * rest
                h1[g, t, pz] = cot[first : first + rest, :]
            h2[pz, t] = cot[pz * share + first_share : (pz + 1) * share, :]
        for ring in x1:
            if hops == nx // 2:
                ring.first()
            elif hops == 1:
                ring.early(0)
            elif hops == -1:
                ring.early(1)
    z2.start()

    half_depth = depth // 2
    parts = 2
    narrow = width // parts

    def piece(t, core):
        block = aligned(t * CORES + core, width)
        cot = jnp.dot(emb_t[...], differ[:, block], preferred_element_type=F32)
        for part in range(parts):
            across = slice(part * narrow, (part + 1) * narrow)
            pc[part, t, core, 0] = cot[:half_depth, across]
            pc[part, t, core, 1] = cot[half_depth:, across]

    def to_sibling(number, t):
        return remote(
            pc.at[:, t, 1 - my_c], sib.at[number], sib_send.at[0], sib_recv.at[number], sibling
        )

    def y_ring_of(part):
        return Ring(
            ny,
            my_y,
            lambda t, half: pc.at[part, t, my_c, half],
            yrecv.at[part],
            y_sems.at[part],
            y_pairs.at[part],
            on_y,
        )

    y_rings = [y_ring_of(part) for part in range(parts)]
    y_at = y_rings[0].at
    near = [1, -1] if ny == 4 else []
    order = [ny // 2] + near + [0]
    for number, hops in enumerate(order):
        t = y_at(hops)
        piece(t, 1 - my_c)
        to_sibling(number, t).start()
        piece(t, my_c)
        to_sibling(number, t).wait_recv()
        for part in range(parts):
            pc[part, t, my_c] = pc[part, t, my_c] + sib[number, part]
        if hops == ny // 2:
            y_rings[0].first()
        elif hops == 1:
            y_rings[0].early(0)
        elif hops == -1:
            y_rings[0].early(1)
    y_rings[1].first()

    def add_up(i, acc):
        lines = aligned(i, 8)
        return acc + qpart[lines, :] * rbc[lines, :]

    code_score = lax.fori_loop(0, crops // 8, add_up, jnp.zeros((8, 128), F32))
    log_total = jnp.log(soft_total) * (1.0 / (nx * nz))
    if crop_blocks != 8:
        log_total = jnp.broadcast_to(jnp.sum(log_total, axis=0, keepdims=True), (8, 128)) / 8.0
    loss_dp = Exchange(ldp, loss_sems.at[0], my_dp, dp_count, on_dp)
    loss_x = Exchange(lx, loss_sems.at[1], my_x, nx, on_x)
    loss_z = Exchange(lz, loss_sems.at[2], my_z, nz, on_z)
    loss_dp.start(log_total - code_score)

    for ring in x1:
        ring.second()
    y_rings[0].second()
    y_rings[1].early(0)
    y_rings[1].early(1)
    for ring, scatter in zip(x1, z1):
        ring.finish()
        scatter.start()
        if ring is x1[0]:
            y_rings[1].second()
    h2[my_z] = z2.finish()
    x2.start()

    def columns(t, core, part):
        first = (t * CORES + core) * width + part * narrow
        return pl.ds(pl.multiple_of(first, narrow), narrow)

    def pull_columns(part):
        block = columns(my_y, my_c, part)
        values = pro[:, block].astype(F32)
        inv = inv_norm(jnp.sum(values * values, axis=0, keepdims=True))
        cots = [pc[part, my_y, my_c, 0], pc[part, my_y, my_c, 1]]
        along = jnp.sum(cots[0] * values[:half_depth, :], axis=0, keepdims=True) + jnp.sum(
            cots[1] * values[half_depth:, :], axis=0, keepdims=True
        )
        factor = PROTOS / math.sqrt(total_crops)
        pull = along * (inv * inv * inv) * factor
        scale = inv * factor
        out_p[0, :, block] = cots[0] * scale - values[:half_depth, :] * pull
        out_p[1, :, block] = cots[1] * scale - values[half_depth:, :] * pull

    def along_y(way, step, half, t, part):
        view = out_p.at[half, :, columns(t, my_c, part)]
        peer = on_y(y_at(1 if way == 0 else -1))
        return remote(view, view, ring_sems.at[5, 0], yg_recv.at[part, way, step, half], peer)

    def hand_on(t, part):
        view = out_p.at[:, :, columns(t, my_c, part)]
        remote(view, view, ring_sems.at[6, 0], ring_sems.at[6, 1], sibling).start()

    def give_y(part):
        y_rings[part].finish()
        pull_columns(part)
        if ny == 4:
            for half in range(2):
                along_y(0, 0, half, my_y, part).start()
                along_y(1, 0, 1 - half, my_y, part).start()
        else:
            along_y(0, 1, 0, my_y, part).start()
            along_y(1, 1, 1, my_y, part).start()
        hand_on(my_y, part)

    give_y(0)

    def pull_rows(cot, first, count):
        values = emb[aligned(my_x * nz + my_z, share), :].astype(F32)
        values = values[first : first + count, :]
        inv = inv_norm(jnp.sum(values * values, axis=1, keepdims=True))
        along = jnp.sum(cot * values, axis=1, keepdims=True)
        factor = math.sqrt(PROTOS)
        out_e[my_x, my_z, pl.ds(first, count)] = cot * (inv * factor) - values * (
            along * (inv * inv * inv) * factor
        )

    late = pl.ds(first_share, rest)
    soon = pl.ds(0, first_share)

    def z_at(hops):
        return lax.rem(my_z + hops + nz, nz)

    def over_x_from(rel):
        view = out_e.at[my_x, z_at(rel), soon]
        for hop in far_first(nx):
            remote(
                view, view, ring_sems.at[1, 0], ring_sems.at[1, 1], on_x(x1[0].at(hop))
            ).start()

    def over_z_at(rel):
        view = out_e.at[my_x, my_z, soon]
        return remote(view, view, ring_sems.at[4, 0], zg_recv.at[rel], on_z(z_at(rel)))

    pull_rows(x2.finish(), first_share, rest)
    for hop in far_first(nx):
        view = out_e.at[my_x, my_z, late]
        remote(
            view, view, ring_sems.at[7, 0], ring_sems.at[7, 1], on_x(x1[0].at(hop))
        ).start()
    give_y(1)
    pull_rows(jnp.concatenate([scatter.finish() for scatter in z1], axis=0), 0, first_share)
    for hop in far_first(nz):
        over_z_at(hop).start()
    over_x_from(0)

    loss_x.start(loss_dp.finish())

    def receive_z(rel):
        view = out_e.at[my_x, z_at(rel), soon]
        remote(view, view, ring_sems.at[4, 0], zg_recv.at[nz - rel], on_z(my_z)).wait_recv()
        over_x_from(rel)

    def send_late():
        arrived(out_e.at[pl.ds(0, nx - 1), 0, late], ring_sems.at[7], on_x(my_x))
        for hop in far_first(nz):
            view = out_e.at[:, my_z, late]
            remote(
                view, view, ring_sems.at[0, 0], ring_sems.at[0, 1], on_z(z_at(hop))
            ).start()

    def receive_y(way, step, half, part):
        t = y_at((-1 if way == 0 else 1) if step == 0 else ny // 2)
        view = out_p.at[half, :, columns(t, my_c, part)]
        remote(
            view, view, ring_sems.at[5, 0], yg_recv.at[part, way, step, half], on_y(my_y)
        ).wait_recv()

    def near_y(part, first):
        if ny == 4:
            for way in range(2):
                half = way if first else 1 - way
                t = y_at(-1 if way == 0 else 1)
                receive_y(way, 0, half, part)
                if first:
                    along_y(way, 1, half, t, part).start()
                else:
                    hand_on(t, part)

    pending = [nz - hop for hop in far_first(nz)]
    near_y(0, True)
    near_y(1, True)
    send_late()
    for rel in pending:
        receive_z(rel)
    near_y(0, False)
    loss_z.start(loss_x.finish())
    near_y(1, False)
    for part in range(parts):
        for way in range(2):
            receive_y(way, 1, way, part)
        hand_on(y_at(ny // 2), part)
    out_l[0, 0] = jnp.sum(loss_z.finish()) / total_crops

    arrived(out_e.at[:, pl.ds(0, nz - 1), late], ring_sems.at[0], on_z(my_z))
    arrived(out_e.at[pl.ds(0, nx - 1), :, soon], ring_sems.at[1], on_x(my_x))
    own = out_p.at[:, :, pl.ds(0, ny * width)]
    arrived(own, ring_sems.at[6], sibling)
    departed(own, ring_sems.at[6], sibling)
    for g in range(groups):
        departed(h1.at[g, pl.ds(0, nx - 1)], x1_sems.at[g], on_x(my_x))
    for ring in (*z1, z2, x2):
        ring.close()
    for part in range(parts):
        departed(pc.at[part, pl.ds(0, ny - 1), 0], y_sems.at[part], on_y(my_y))
    remote(pc.at[:, :, 0], pc.at[:, :, 0], sib_send.at[0], sib_recv.at[0], sibling).wait_send()
    departed(out_p.at[:, :, pl.ds(0, (ny - 1) * width)], ring_sems.at[5], on_y(my_y))
    departed(out_e.at[pl.ds(0, nx - 1), 0, late], ring_sems.at[7], on_x(my_x))
    departed(out_e.at[0, pl.ds(0, nz - 1), soon], ring_sems.at[4], on_z(my_z))
    departed(out_e.at[pl.ds(0, nx - 1), :, soon], ring_sems.at[1], on_x(my_x))
    departed(out_e.at[:, pl.ds(0, nz - 1), late], ring_sems.at[0], on_z(my_z))


def local(sizes, embeddings, queue, prototypes, pairing):
    ny, nx, nz = sizes
    dp_count = ny * CORES
    crops, depth = embeddings.shape
    rows = crops + queue.shape[0]
    cols = prototypes.shape[1]
    width = cols // dp_count
    share = crops // (nx * nz)
    rest = share // 4
    row_blocks, crop_blocks, lane_blocks = rows // 128, crops // 128, cols // 128
    half = depth // 2
    tile = 256
    dma = pltpu.SemaphoreType.DMA
    vmem = pltpu.VMEM
    scratch = [
        vmem((crops, depth), BF16),
        vmem((rows - crops, depth), BF16),
        vmem((depth, cols), BF16),
        vmem((1, crops), jnp.int32),
        vmem((rows, cols), F32),
        vmem((crops, cols), F32),
        vmem((crops, cols), F32),
        vmem((rows, depth), BF16),
        vmem((crops, depth), BF16),
        vmem((depth, cols), BF16),
        vmem((depth, crops), BF16),
        vmem((cols, depth), BF16),
        vmem((crops, cols), BF16),
        vmem((cols // 1024, 8, 1024), F32),
        vmem((row_blocks, 128), F32),
        vmem((crops, 128), F32),
        vmem((rows, 128), F32),
        vmem((crops, 128), F32),
        vmem((crops, 128), F32),
        vmem((ITERS, dp_count, lane_blocks, 128), F32),
        vmem((ITERS, nx, row_blocks, 128), F32),
        vmem((ITERS, nz, row_blocks, 128), F32),
        vmem((nx, crop_blocks, 128), F32),
        vmem((nz, crop_blocks, 128), F32),
        vmem((dp_count, 8, 128), F32),
        vmem((nx, 8, 128), F32),
        vmem((nz, 8, 128), F32),
        vmem((2, ny, CORES, 2, half, width // 2), F32),
        vmem((ny, 2, 2, half, width // 2), F32),
        vmem((2, 2, 2, 2, half, width // 2), F32),
        vmem((3, nx, nz, rest, depth), F32),
        vmem((nz, nx, rest, depth), F32),
        vmem((3, 2, 2, 2, nz // 2, rest, depth), F32),
        vmem((3, nz - 1, rest, depth), F32),
        vmem((nz - 1, nx, rest, depth), F32),
        vmem((nx - 1, rest, depth), F32),
        dma((4,)),
        dma((ITERS, 2)),
        dma((ITERS, 2, 2)),
        dma((ITERS, 2, 2)),
        dma((2, 2)),
        dma((3, 2)),
        dma((1,)),
        dma((ny,)),
        dma((2, 2)),
        dma((2, 2, 2)),
        dma((8, 2)),
        dma((3, 2)),
        dma((3, 2, 2)),
        dma((3, 2)),
        dma((2, 2, 2, 2)),
        dma((nz,)),
    ]
    in_vmem = pl.BlockSpec(memory_space=pltpu.VMEM)
    anywhere = pl.BlockSpec(memory_space=pl.ANY)
    grad_embed, grad_proto, loss = pl.pallas_call(
        functools.partial(kernel, sizes),
        out_shape=(
            pltpu.VMEM((nx, nz, share, depth), F32),
            pltpu.VMEM((2, half, cols), F32),
            jax.ShapeDtypeStruct((1, 1), F32),
        ),
        in_specs=[anywhere] * 4,
        out_specs=(in_vmem, in_vmem, pl.BlockSpec(memory_space=pltpu.SMEM)),
        scratch_shapes=scratch,
        compiler_params=pltpu.CompilerParams(
            collective_id=0, has_side_effects=True, vmem_limit_bytes=59 * 1024 * 1024
        ),
    )(embeddings, queue, prototypes, pairing.reshape(1, crops))
    return (
        grad_embed.reshape(crops, depth),
        grad_proto.reshape(depth, cols),
        loss.reshape(()),
    )


def solution(mesh):
    nx = ALONG_X
    sizes = (mesh.shape["dp"] // CORES, nx, mesh.shape["proto"] // nx)
    return jax.shard_map(
        functools.partial(local, sizes),
        mesh=mesh,
        in_specs=(P("dp", None), P("dp", None), P(None, "proto"), P("dp")),
        out_specs=(P("dp", None), P(None, "proto"), P()),
        check_vma=False,
    )
```
